32 devices in a mesh: groups: 1, cand: 32 (over z, y, x, core).
Axes of the slice: x: 2, y: 2, z: 4, core: 2. Of those that a mesh axis runs over, the one named last changes fastest.
Arguments:
- users: bfloat16 [128, 1024], P(('groups', 'cand')), may hold values from -6 to 6
- items: bfloat16 [32768, 1024], P(('groups', 'cand')), may hold values from -6 to 6
- probes: int32 [128, 32], P(('groups', 'cand')), may hold values from 0 to 63, all different within a row; in each aligned block of 4 rows (0 to 3, 4 to 7, ...) at most 4 rows name the same one
- gate_weight: bfloat16 [64, 64], replicated, may hold values from -0.75 to 0.75
- gate_bias: float32 [64], replicated, may hold values from -2 to 2
- cross_weight: bfloat16 [3, 1024, 1024], replicated, may hold values from -0.09375 to 0.09375
- cross_bias: float32 [3, 1024], replicated, may hold values from -0.5 to 0.5
- out_weight: float32 [1024], replicated, may hold values from -0.1875 to 0.1875
- row_device: int32 [24576, 1], P(('groups', 'cand')), may hold values from 0 to 31; in each aligned block of 768 rows (0 to 767, 768 to 1535, ...) at most 48 rows name the same one
- row_item: int32 [24576], P(('groups', 'cand')), may hold values from 0 to 1023
- row_request: int32 [24576], P(('groups', 'cand')), may hold values from 0 to 127
Outputs:
- top_scores: float32 [128, 96], P(('groups', 'cand'))
- rerank: float32 [24576], P(('groups', 'cand'))
The draws below stay inside these ranges and needn't reach their ends.
Inputs may be any that keep to these rules, and one draw needn't show every extreme that they name: `probes`: each row names 32 different clusters. Among the requests of one index of cand, no cluster is named by more than 4 of them, a bound that some block reaches. `row_device`: among the rows of one index of cand, no index is named more than 48 times, a bound that some block reaches.
All inputs are finite; a program needn't handle non-finite values.
Results may differ from the reference program's by a relative error of at most 0.0037.
Values may be sent and summed in bfloat16 or wider, within the bound.
No kernel may reach another device: no remote copies, remote signals or barrier semaphores. Data moves between devices by JAX's collectives and lax.ppermute only.
A program may use at most 128 MiB of HBM per device.

```python
import math
import jax
import jax.numpy as jnp
import numpy as np
from jax import lax

EMB = 8
D = 128
P_SIZE = 64
WIDTH = 1024
TILE = 512
PROBES = 32
KEEP = 96
LAYERS = 3
CL_DEV = 2
REQ_DEV = 4
ROWS_DEV = 768
CLUSTERS = 64
ITEMS = 32768
REQUESTS = 128
ROWS = 24576
MOST = 4
FCAP = 48
N_CAND = 32


def touch_ends(array, key, smallest, high):
    dims = array.shape
    spot = [jax.random.randint(jax.random.fold_in(key, axis), (), 0, dims[axis]) for axis in range(len(dims))]
    array = array.at[tuple(spot)].set(smallest)
    longest = dims.index(max(dims))
    spot[longest] = (spot[longest] + 1) % dims[longest]
    return array.at[tuple(spot)].set(high)


def shard_levels(key, shape, split, low, high):
    factor_of, own = 1.0, jax.random.fold_in(key, 6)
    for position, blocks in split:
        draws = jnp.exp(jax.random.uniform(jax.random.fold_in(own, position), (blocks,), jnp.float32, low / len(split), high / len(split)))
        factor_of = factor_of * jnp.repeat(draws, shape[position] // blocks).reshape([-1 if axis == position else 1 for axis in range(len(shape))])
    return factor_of


def shared_out(key, own, number, rows, count, top, bound, slope):
    order = jax.random.permutation(key, count)
    packed, usual = load_shares(count, rows * top, bound, slope, True), load_shares(count, rows * top, bound, slope, False)
    places = jnp.arange(count)

    def named(sizes, rotation):
        used = int((sizes > 0).sum())
        fixed = max(1, used // 4)
        passed = fixed + (places - fixed + rotation * (used - fixed)) % max(1, count - fixed)
        return jnp.zeros((count,), jnp.int32).at[order[jnp.where(places < fixed, places, passed)]].set(jnp.asarray(sizes, jnp.int32))

    sizes = jnp.where(number % 4 == 0, named(packed, number // 4), named(usual, number - number // 4 - 1))
    mixed = jax.random.permutation(jax.random.fold_in(own, 3), count)
    source_of, taker = mixed[0:count // 2 * 2:2], mixed[1:count // 2 * 2:2]
    slack = jnp.minimum(sizes[source_of] - 1, bound - sizes[taker]) // 2
    slack = jnp.where((source_of == order[0]) | (taker == order[0]) | (sizes[taker] == 0), 0, jnp.maximum(slack, 0))
    passed = jax.random.randint(jax.random.fold_in(own, 4), (count // 2,), 0, 1 << 20) % (slack + 1)
    sizes = sizes.at[source_of].add(-passed).at[taker].add(passed)
    members = jnp.searchsorted(jnp.cumsum(sizes), jnp.arange(rows * top), side="right").astype(jnp.int32)
    grid = members.reshape(top, rows).T
    grid = grid[jax.random.permutation(jax.random.fold_in(own, 1), rows)]
    rotation = jax.random.randint(jax.random.fold_in(own, 2), (rows, 1), 0, top)
    return jnp.take_along_axis(grid, (jnp.arange(top)[None, :] + rotation) % top, axis=1)


def load_shares(count, total, most, skew, full):
    loads = [(1 << 20) // math.isqrt(grade ** skew) + 1 for grade in range(1, count + 1)]
    largest = most if full else min(most, max(-(-total // count), total * loads[0] // sum(loads)))
    least = 1 if total - largest >= count - 1 else 0
    given, spare = [largest] + [least] * (count - 1), total - largest - least * (count - 1)
    while spare > 0:
        candidates = [i for i in range(1, count) if given[i] < largest] or [i for i in range(1, count) if given[i] < most]
        pool, left = sum([loads[i] for i in candidates]), spare
        for i in candidates:
            extra = min(most - given[i], max(1, left * loads[i] // pool), spare)
            given[i] = given[i] + extra
            spare = spare - extra
    return np.array(given)


def normal_values(own_key, dims, spread, limit, cuts=(), held_as=jnp.bfloat16):
    result = spread * jax.random.normal(own_key, dims, jnp.float32)
    if cuts:
        result = result * shard_levels(own_key, dims, cuts, -0.22, 0.18)
    return jnp.clip(result, -limit, limit).astype(held_as)


def setup_inputs(seed: int = 0, part: int = 0) -> dict:
    keys = jax.random.split(jax.random.key(seed), 12)
    part_keys = jax.random.split(jax.random.fold_in(keys[11], part), 12)
    users = normal_values(part_keys[0], (REQUESTS, WIDTH), 1.0, 6.0, ((0, 32),))
    items = normal_values(part_keys[1], (ITEMS, WIDTH), 1.0, 6.0, ((0, 32),))
    probes_keys = jax.random.split(jax.random.fold_in(part_keys[2], 1), REQUESTS // REQ_DEV)
    probes_turns = jax.random.permutation(jax.random.fold_in(part_keys[2], 3), REQUESTS // REQ_DEV)
    probes = jax.vmap(lambda own, number: shared_out(jax.random.fold_in(part_keys[2], 2), own, number, REQ_DEV, CLUSTERS, PROBES, MOST, 2))(probes_keys, probes_turns).reshape((REQUESTS, PROBES))
    gate_weight = normal_values(keys[3], (P_SIZE, P_SIZE), P_SIZE ** -0.5, 0.75)
    gate_bias = jnp.clip(jax.random.uniform(keys[4], (P_SIZE,), jnp.float32, -2.0, 2.0), -2.0, 2.0)
    cross_weight = normal_values(keys[5], (LAYERS, WIDTH, WIDTH), (4 * WIDTH) ** -0.5, 0.09375)
    cross_bias = jnp.clip(jax.random.uniform(keys[6], (LAYERS, WIDTH), jnp.float32, -0.5, 0.5), -0.5, 0.5)
    out_weight = normal_values(keys[7], (WIDTH,), WIDTH ** -0.5, 0.1875, (), jnp.float32)
    row_device_keys = jax.random.split(jax.random.fold_in(part_keys[8], 1), ROWS // ROWS_DEV)
    row_device_turns = jax.random.permutation(jax.random.fold_in(part_keys[8], 3), ROWS // ROWS_DEV)
    row_device = jax.vmap(lambda own, number: shared_out(jax.random.fold_in(part_keys[8], 2), own, number, ROWS_DEV, N_CAND, 1, FCAP, 2))(row_device_keys, row_device_turns).reshape((ROWS, 1))
    row_item = touch_ends(jax.random.randint(part_keys[9], (ROWS,), 0, CL_DEV * TILE), jax.random.fold_in(part_keys[9], 1), 0, (CL_DEV * TILE) - 1).astype(jnp.int32)
    row_request = touch_ends(jax.random.randint(part_keys[10], (ROWS,), 0, REQUESTS), jax.random.fold_in(part_keys[10], 1), 0, REQUESTS - 1).astype(jnp.int32)
    return dict(users=users, items=items, probes=probes, gate_weight=gate_weight, gate_bias=gate_bias, cross_weight=cross_weight, cross_bias=cross_bias, out_weight=out_weight, row_device=row_device, row_item=row_item, row_request=row_request)


def mixture_scores(queries, item_tile, gate_weight, gate_bias):
    slot_count = queries.shape[0]
    tile_rows = item_tile.shape[0]
    views = queries.astype(jnp.float32).reshape(slot_count, EMB, D)
    targets = item_tile.astype(jnp.float32).reshape(tile_rows, EMB, D)
    pair_dots = jnp.einsum('sid,njd->sijn', views, targets) * (1.0 / math.sqrt(D))
    pair_dots = pair_dots.reshape(slot_count, EMB * EMB, tile_rows).astype(jnp.bfloat16)
    logits = jnp.einsum('spn,pq->sqn', pair_dots.astype(jnp.float32), gate_weight.astype(jnp.float32)) + gate_bias[None, :, None]
    weights = jax.nn.softplus(logits)
    return lax.optimization_barrier(jnp.sum(weights * pair_dots.astype(jnp.float32), axis=1)) / (1.0 + lax.optimization_barrier(jnp.sum(weights, axis=1)))

def pair_scores(user_rows, item_rows, gate_weight, gate_bias):
    row_count = user_rows.shape[0]
    views = user_rows.astype(jnp.float32).reshape(row_count, EMB, D)
    targets = item_rows.astype(jnp.float32).reshape(row_count, EMB, D)
    pair_dots = jnp.einsum('rid,rjd->rij', views, targets) * (1.0 / math.sqrt(D))
    pair_dots = pair_dots.reshape(row_count, EMB * EMB).astype(jnp.bfloat16)
    logits = jnp.dot(pair_dots, gate_weight, preferred_element_type=jnp.float32) + gate_bias
    weights = jax.nn.softplus(logits)
    return lax.optimization_barrier(jnp.sum(weights * pair_dots.astype(jnp.float32), axis=1)) / (1.0 + lax.optimization_barrier(jnp.sum(weights, axis=1)))

def cross_scores(user_rows, item_rows, gate_weight, gate_bias, cross_weight, cross_bias, out_weight):
    cross_input = user_rows.astype(jnp.float32) + item_rows.astype(jnp.float32)
    cross_state = cross_input
    for layer_index in range(LAYERS):
        hidden = jnp.dot(cross_state.astype(jnp.bfloat16), cross_weight[layer_index], preferred_element_type=jnp.float32) + cross_bias[layer_index]
        cross_state = cross_input * hidden + cross_state
    return pair_scores(user_rows, item_rows, gate_weight, gate_bias) + lax.optimization_barrier(jnp.sum(cross_state * out_weight, axis=1))

def reference(users, items, probes, gate_weight, gate_bias, cross_weight, cross_bias, out_weight, row_device, row_item, row_request):
    item_tiles = items.reshape(CL_DEV * N_CAND, TILE, EMB * D)

    def one_request(operands):
        query, chosen = operands
        gathered = jnp.take(item_tiles, chosen.astype(jnp.int32), axis=0).reshape(PROBES * TILE, EMB * D)
        values = mixture_scores(query[None, :], gathered, gate_weight, gate_bias)[0]
        return lax.top_k(values, KEEP)[0]
    top_scores = lax.map(one_request, (users, probes))
    item_index = (row_device[:, 0] * (CL_DEV * TILE) + row_item).astype(jnp.int32)

    def one_block(operands):
        wanted, asked = operands
        user_rows = jnp.take(users, asked.astype(jnp.int32), axis=0)
        item_rows = jnp.take(items, wanted.astype(jnp.int32), axis=0)
        return cross_scores(user_rows, item_rows, gate_weight, gate_bias, cross_weight, cross_bias, out_weight)
    rerank = lax.map(one_block, (item_index.reshape(N_CAND, ROWS_DEV), row_request.reshape(N_CAND, ROWS_DEV))).reshape(-1)
    return (top_scores, rerank)
```

```python
import functools
import math

import jax
import jax.numpy as jnp
from jax import lax
from jax.experimental import pallas as pl
from jax.experimental.pallas import tpu as pltpu
from jax.sharding import PartitionSpec as P

EMB = 8
D = 128
PAIRS = EMB * EMB
PROBES = 32
KEEP = 96
CL_DEV = 2
REQ_DEV = 4
LANES = 128
TILE_COLS = 256
GROUP = 4
BASE = 32
LOG2E = math.log2(math.e)
SCALE = 1.0 / math.sqrt(D)
VMEM = 56 * 1024 * 1024

F32 = jnp.float32
BF16 = jnp.bfloat16
NT = (((1,), (1,)), ((), ()))


def iota(shape, dim):
    return lax.broadcasted_iota(jnp.int32, shape, dim)


def dot(a, b):
    return jnp.dot(a, b, preferred_element_type=F32)


def dot_nt(a, b):
    return lax.dot_general(a, b, NT, preferred_element_type=F32)


def ones_where(cond):
    return jnp.where(cond, 1.0, 0.0).astype(BF16)


def split_two(x):
    high = x.astype(BF16)
    return high, (x - high.astype(F32)).astype(BF16)


def plan_kernel(owner_ref, item_ref, request_ref, probes_ref, gate_ref, bias_ref,
                codes_ref, place_ref, gate_out, bias_out):
    rows = owner_ref.shape[1]
    size = codes_ref.shape[0]
    at = owner_ref[...] == iota((size, rows), 0)
    at_one = ones_where(at)
    before = ones_where(iota((rows, rows), 0) < iota((rows, rows), 1))
    rank = dot(at_one, before)
    place = jnp.sum(jnp.where(at, rank, 0.0), axis=0, keepdims=True).astype(jnp.int32)
    place_ref[...] = place
    slots = ones_where(place == iota((LANES, rows), 0))
    item = item_ref[...]
    values = (item // BASE, item % BASE, request_ref[...])
    spread = jnp.concatenate(
        [jnp.where(at, value.astype(F32), 0.0).astype(BF16) for value in values], axis=0
    )
    codes = dot_nt(spread, slots)
    codes_ref[:, :LANES] = (codes[:size] * BASE + codes[size : 2 * size]).astype(jnp.int32)
    codes_ref[:, LANES : 2 * LANES] = codes[2 * size :].astype(jnp.int32)
    requests, probes = probes_ref.shape
    lane = iota((size, LANES), 1)
    masks = jnp.zeros((size, LANES), F32)
    for cluster in range(CL_DEV):
        ids = iota((size, probes), 0) * CL_DEV + cluster
        for request in range(requests):
            hit = jnp.where(probes_ref[request : request + 1, :] == ids, 1.0, 0.0)
            any_hit = jnp.max(hit, axis=1, keepdims=True)
            masks = jnp.where(lane == cluster * requests + request, any_hit, masks)
    codes_ref[:, 2 * LANES :] = masks.astype(jnp.int32)
    side = GROUP * PAIRS
    step = GROUP * EMB
    row, col = iota((side, PAIRS), 0), iota((side, PAIRS), 1)
    select = ones_where((row % EMB) * EMB + row // step == col)
    part = dot_nt(select, gate_ref[...]).astype(BF16)
    full = dot_nt(part, select)
    same = (iota((side, side), 0) // EMB) % GROUP == (iota((side, side), 1) // EMB) % GROUP
    gate_out[...] = jnp.where(same, full, 0.0).astype(BF16)
    row, col = iota((PAIRS, PAIRS), 0), iota((PAIRS, PAIRS), 1)
    order = (row % EMB) * EMB + row // EMB == col
    column = jnp.sum(jnp.where(order, bias_ref[...], 0.0), axis=1, keepdims=True)
    bias_out[...] = jnp.broadcast_to(column, bias_out.shape)


def plan(owner, item, request, probes, gate_weight, gate_bias, size):
    rows = owner.shape[1]
    return pl.pallas_call(
        plan_kernel,
        out_shape=(
            jax.ShapeDtypeStruct((size, 3 * LANES), jnp.int32),
            jax.ShapeDtypeStruct((1, rows), jnp.int32),
            jax.ShapeDtypeStruct((GROUP * PAIRS, GROUP * PAIRS), BF16),
            jax.ShapeDtypeStruct((PAIRS, LANES), F32),
        ),
        compiler_params=pltpu.CompilerParams(vmem_limit_bytes=VMEM),
        name="plan",
    )(owner, item, request, probes, gate_weight, gate_bias)


def score_kernel(query_ref, items_ref, gate_ref, bias_ref, scores_ref,
                 dots_a, dots_b, logits_a, logits_b, num_ref, den_ref):
    query_rows = query_ref.shape[0]
    tiles = items_ref.shape[0] // TILE_COLS
    step = GROUP * EMB
    groups = query_rows // step
    row_blocks = query_rows // TILE_COLS

    def piece(tile, index, out):
        j, block = index // row_blocks, index % row_blocks
        start = pl.multiple_of(block * TILE_COLS, TILE_COLS)
        lanes = pl.multiple_of(j * D, D)
        values = dot_nt(
            query_ref[pl.ds(start, TILE_COLS), :],
            items_ref[tile * TILE_COLS : (tile + 1) * TILE_COLS, pl.ds(lanes, D)],
        )
        out[j, pl.ds(start, TILE_COLS), :] = (values * SCALE).astype(BF16)

    def gate(dots, group, out):
        start = pl.multiple_of(group * step, step)
        part = dots[:, pl.ds(start, step), :].reshape(GROUP * PAIRS, TILE_COLS)
        out[...] = dot(gate_ref[...], part)

    def mix(dots, group, logits):
        start = pl.multiple_of(group * step, step)
        num = jnp.zeros((step, TILE_COLS), F32)
        den = jnp.zeros((step, TILE_COLS), F32)
        for j in range(EMB):
            bias = bias_ref[j * EMB : (j + 1) * EMB, :]
            bias = jnp.concatenate([jnp.concatenate([bias] * GROUP, axis=0)] * 2, axis=1)
            logit = logits[j * step : (j + 1) * step, :] + bias
            power = jnp.exp2(jnp.minimum(logit * LOG2E, 126.0))
            weight = jnp.maximum(jnp.log(1.0 + power), logit)
            den = den + weight
            num = num + weight * dots[j, pl.ds(start, step), :].astype(F32)
        for half in range(TILE_COLS // LANES):
            lanes = slice(half * LANES, (half + 1) * LANES)
            num_ref[half, pl.ds(start, step), :] = num[:, lanes]
            den_ref[half, pl.ds(start, step), :] = den[:, lanes]

    buffers = (dots_a, dots_b)

    @pl.loop(0, groups)
    def _(index):
        piece(0, index, dots_a)

    for tile in range(tiles):
        dots, ahead = buffers[tile % 2], buffers[(tile + 1) % 2]
        gate(dots, 0, logits_a)

        @pl.loop(0, groups // 2)
        def _(pair):
            first = pair * 2
            if tile + 1 < tiles:
                piece(tile + 1, first, ahead)
                piece(tile + 1, first + 1, ahead)
            gate(dots, first + 1, logits_b)
            mix(dots, first, logits_a)
            gate(dots, jnp.minimum(first + 2, groups - 1), logits_a)
            mix(dots, first + 1, logits_b)

        for half in range(TILE_COLS // LANES):
            num = jnp.zeros((query_rows // EMB, LANES), F32)
            den = jnp.ones((query_rows // EMB, LANES), F32)
            for i in range(EMB):
                num = num + num_ref[half, pl.ds(i, query_rows // EMB, stride=EMB), :]
                den = den + den_ref[half, pl.ds(i, query_rows // EMB, stride=EMB), :]
            start = tile * TILE_COLS + half * LANES
            scores_ref[start : start + LANES, :] = (num / den).T


def score(queries, items, gate_full, bias_full):
    query_rows, item_rows = queries.shape[0], items.shape[0]
    return pl.pallas_call(
        score_kernel,
        out_shape=jax.ShapeDtypeStruct((item_rows, query_rows // EMB), F32),
        scratch_shapes=[
            pltpu.VMEM((EMB, query_rows, TILE_COLS), BF16),
            pltpu.VMEM((EMB, query_rows, TILE_COLS), BF16),
            pltpu.VMEM((GROUP * PAIRS, TILE_COLS), F32),
            pltpu.VMEM((GROUP * PAIRS, TILE_COLS), F32),
            pltpu.VMEM((TILE_COLS // LANES, query_rows, LANES), F32),
            pltpu.VMEM((TILE_COLS // LANES, query_rows, LANES), F32),
        ],
        compiler_params=pltpu.CompilerParams(vmem_limit_bytes=VMEM),
        name="score",
    )(queries, items, gate_full, bias_full)


def batcher(count):
    pairs = []
    p = 1
    while p < count:
        k = p
        while k >= 1:
            for j in range(k % p, count - k, 2 * k):
                for i in range(min(k, count - j - k)):
                    if (i + j) // (2 * p) == (i + j + k) // (2 * p):
                        pairs.append((i + j, i + j + k))
            k //= 2
        p *= 2
    return pairs


def order_pair(values, i, j):
    values[i], values[j] = jnp.maximum(values[i], values[j]), jnp.minimum(values[i], values[j])


def clean(values):
    stride = len(values) // 2
    while stride:
        for i in range(len(values)):
            if not i & stride:
                order_pair(values, i, i + stride)
        stride //= 2


def clean_block(load, store, start, count):
    values = [load(start + i) for i in range(count)]
    clean(values)
    for i in range(count):
        store(start + i, values[i])


def sort_all(load, store, load_sorted, total, block):
    for start in range(0, total, block):
        values = [load(start + i) for i in range(block)]
        for i, j in batcher(block):
            order_pair(values, i, j)
        for i in range(block):
            store(start + i, values[i])
    size = 2 * block
    while size <= total:
        for start in range(0, total, size):
            if size == 2 * block:
                upper, lower = [], []
                for i in range(block):
                    a, b = load_sorted(start + i), load_sorted(start + size - 1 - i)
                    upper.append(jnp.maximum(a, b))
                    lower.append(jnp.minimum(a, b))
                for offset, values in ((0, upper), (block, lower[::-1])):
                    clean(values)
                    for i in range(block):
                        store(start + offset + i, values[i])
            else:
                half, quarter = size // 2, size // 4
                for i in range(quarter):
                    spots = (i, i + quarter, size - 1 - i - quarter, size - 1 - i)
                    values = [load_sorted(start + spot) for spot in spots]
                    order_pair(values, 0, 3)
                    order_pair(values, 1, 2)
                    order_pair(values, 0, 1)
                    order_pair(values, 2, 3)
                    for spot, value in zip(spots, values):
                        store(start + spot, value)
                for offset in range(0, size, quarter):
                    clean_block(load_sorted, store, start + offset, quarter)
        size *= 2


def merge_top(load, store, load_merged, partner, total):
    quarter = total // 4
    done = {}
    for i in range(quarter):
        spots = [i, i + quarter, i + 2 * quarter, i + 3 * quarter]
        values = [jnp.maximum(load(spot), partner(load(total - 1 - spot))) for spot in spots]
        order_pair(values, 0, 2)
        order_pair(values, 1, 3)
        order_pair(values, 0, 1)
        order_pair(values, 2, 3)
        for spot, value in zip(spots, values):
            store(spot, value)
    for offset in range(0, total, quarter):
        clean_block(load_merged, store, offset, quarter)


def rank_kernel(scores_ref, query_ref, items_ref, codes_ref, weight_hbm, bias_ref, out_weight_ref,
                result_ref, weight_ref, query_f32, user_ref, sort_a, sort_b, best_ref, weight_sem,
                *, fetch):
    copy = pltpu.make_async_copy(weight_hbm, weight_ref, weight_sem)
    copy.start()
    size = codes_ref.shape[0]
    item_rows, requests = scores_ref.shape
    local = requests // size
    best_of(scores_ref, codes_ref, result_ref, sort_a, sort_b, best_ref, local)

    query_f32[...] = query_ref[...].astype(F32)
    for i in range(EMB):
        user_ref[:, i * D : (i + 1) * D] = query_f32[pl.ds(i, requests, stride=EMB), :].astype(BF16)
    scores_high, scores_low = split_two(scores_ref[...])
    copy.wait()
    total = size * fetch
    block = total // 3
    code_item = codes_ref[:, :LANES]
    digits = jnp.concatenate(
        [code_item // BASE, code_item % BASE, codes_ref[:, LANES : 2 * LANES]], axis=1
    ).astype(F32).astype(BF16)
    answer = jnp.zeros((size, LANES), F32)
    for start in range(0, total, block):
        def source_of(shape, dim):
            row = (iota(shape, dim) + start).astype(F32)
            return jnp.floor((row + 0.5) * (1.0 / fetch))

        from_source = ones_where(source_of((block, size), 0) == iota((block, size), 1).astype(F32))
        taken = dot(from_source, digits)
        slot = iota((block, LANES), 0) + start - source_of((block, LANES), 0).astype(jnp.int32) * fetch
        mine = slot == iota((block, LANES), 1)
        item = jnp.sum(
            jnp.where(mine, taken[:, :LANES] * BASE + taken[:, LANES : 2 * LANES], 0.0),
            axis=1, keepdims=True,
        ).astype(jnp.int32)
        request = jnp.sum(
            jnp.where(mine, taken[:, 2 * LANES :], 0.0), axis=1, keepdims=True
        ).astype(jnp.int32)
        pick_item = ones_where(item == iota((block, item_rows), 1))
        asked = request == iota((block, requests), 1)
        pick_user = ones_where(asked)
        first = dot(pick_item, items_ref[...]) + dot(pick_user, user_ref[...])
        state = first
        for layer in range(weight_ref.shape[0]):
            hidden = dot(state.astype(BF16), weight_ref[layer]) + bias_ref[layer : layer + 1, :]
            state = first * hidden + state
        mixed = dot(pick_item, scores_high) + dot(pick_item, scores_low)
        mixed = jnp.where(asked, mixed, 0.0)
        weighted = state * out_weight_ref[...]
        partial = sum(
            [weighted[:, i * LANES : (i + 1) * LANES] for i in range(1, weighted.shape[1] // LANES)],
            weighted[:, :LANES],
        )
        for i in range(requests // LANES):
            partial = partial + mixed[:, i * LANES : (i + 1) * LANES]
        column = jnp.sum(partial, axis=1, keepdims=True)
        placed = jnp.where(mine, column, 0.0)
        to_source = ones_where(source_of((size, block), 1) == iota((size, block), 0).astype(F32))
        high, rest = split_two(placed)
        middle, low = split_two(placed - high.astype(F32))
        answer = answer + (dot(to_source, high) + (dot(to_source, middle) + dot(to_source, low)))
    result_ref[:, local * LANES :] = answer


def best_of(scores_ref, codes_ref, result_ref, sort_a, sort_b, best_ref, local):
    size = codes_ref.shape[0]
    item_rows, requests = scores_ref.shape
    lists = item_rows // EMB
    masks = codes_ref[:, 2 * LANES :].astype(F32).astype(BF16)
    lane, from_row = iota((LANES, requests), 1), iota((LANES, requests), 0)
    source = iota((size, requests), 1) // local == iota((size, requests), 0)
    allowed = []
    for cluster in range(CL_DEV):
        spread = dot(masks, ones_where(from_row == cluster * local + lane % local))
        allowed.append(jnp.sum(jnp.where(source, spread, 0.0), axis=0, keepdims=True) > 0.5)
    for chunk in range(requests // LANES):
        lanes = slice(chunk * LANES, (chunk + 1) * LANES)
        fits = [jnp.broadcast_to(a[:, lanes], (EMB, LANES)) for a in allowed]

        def load(i):
            values = scores_ref[i * EMB : (i + 1) * EMB, lanes]
            return jnp.where(fits[i * CL_DEV // lists], values, -jnp.inf)

        def reader(ref):
            return lambda i: ref[i]

        def writer(ref):
            def store(i, value):
                ref[i] = value
            return store

        sort_all(load, writer(sort_a), reader(sort_a), lists, 32)
        held, other = sort_a, sort_b
        shift = EMB // 2
        while shift:
            merge_top(
                reader(held), writer(other), reader(other),
                functools.partial(pltpu.roll, shift=shift, axis=0), lists,
            )
            held, other = other, held
            shift //= 2
        for i in range(lists):
            best_ref[i : i + 1, :] = held[i][:1, :]
        best_ref[...] = best_ref[...].T
        per_chunk = LANES // local
        for r in range(local):
            result_ref[chunk * per_chunk : (chunk + 1) * per_chunk, r * LANES : (r + 1) * LANES] = (
                best_ref[pl.ds(r, per_chunk, stride=local), :]
            )


def rank(scores, queries, items, codes, cross_weight, cross_bias, out_weight, local, fetch):
    size = codes.shape[0]
    requests = scores.shape[1]
    vmem = pl.BlockSpec(memory_space=pltpu.VMEM)
    return pl.pallas_call(
        functools.partial(rank_kernel, fetch=fetch),
        out_shape=jax.ShapeDtypeStruct((size, (local + 1) * LANES), F32),
        in_specs=[vmem, vmem, vmem, vmem, pl.BlockSpec(memory_space=pl.ANY), vmem, vmem],
        out_specs=vmem,
        scratch_shapes=[
            pltpu.VMEM(cross_weight.shape, BF16),
            pltpu.VMEM(queries.shape, F32),
            pltpu.VMEM((requests, EMB * D), BF16),
            pltpu.VMEM((items.shape[0] // EMB, EMB, LANES), F32),
            pltpu.VMEM((items.shape[0] // EMB, EMB, LANES), F32),
            pltpu.VMEM((LANES, LANES), F32),
            pltpu.SemaphoreType.DMA,
        ],
        compiler_params=pltpu.CompilerParams(vmem_limit_bytes=VMEM),
        name="rank",
    )(scores, queries, items, codes, cross_weight, cross_bias, out_weight)


def merge_kernel(back_ref, owner_ref, place_ref, top_ref, rerank_ref, list_ref, merge_a, merge_b):
    size = back_ref.shape[0]
    local = back_ref.shape[1] // LANES - 1
    rows = owner_ref.shape[1]
    at = owner_ref[...] == iota((size, rows), 0)
    slots = ones_where(place_ref[...] == iota((LANES, rows), 0))
    answer = back_ref[:, local * LANES :]
    high, rest = split_two(answer)
    middle, low = split_two(answer - high.astype(F32))
    spread = dot(high, slots) + (dot(middle, slots) + dot(low, slots))
    rerank_ref[...] = jnp.sum(jnp.where(at, spread, 0.0), axis=0, keepdims=True)

    for r in range(local):
        list_ref[pl.ds(r, size, stride=local), :] = back_ref[:, r * LANES : (r + 1) * LANES]
    chunks = size * local // LANES
    merge_a[...] = list_ref[...].T

    def reader(ref, chunk=0):
        return lambda i: ref[i : i + 1, chunk * LANES : (chunk + 1) * LANES]

    def writer(ref):
        def store(i, value):
            ref[i : i + 1, :LANES] = value
        return store

    held, other = merge_a, merge_b
    while chunks > 1:
        half = chunks // 2
        for chunk in range(half):
            take = slice(chunk * LANES, (chunk + 1) * LANES)

            def load(i, ref=held, first=chunk, second=chunk + half):
                return ref[i : i + 1, first * LANES : (first + 1) * LANES]

            def store(i, value, ref=other, take=take):
                ref[i : i + 1, take] = value

            def read(i, ref=other, take=take):
                return ref[i : i + 1, take]

            merge_pairs(
                load,
                lambda i, ref=held, c=chunk + half: ref[i : i + 1, c * LANES : (c + 1) * LANES],
                store, read, LANES,
            )
        held, other = other, held
        chunks = half
    shift = LANES // 2
    while shift >= local:
        merge_top(
            reader(held), writer(other), reader(other),
            functools.partial(pltpu.roll, shift=LANES - shift, axis=1), LANES,
        )
        held, other = other, held
        shift //= 2
    top_ref[...] = held[:, :LANES].T[:local, :KEEP]


def merge_pairs(load, load_other, store, load_merged, total):
    for i in range(total):
        store(i, jnp.maximum(load(i), load_other(total - 1 - i)))
    quarter = total // 4
    for i in range(quarter):
        spots = [i, i + quarter, i + 2 * quarter, i + 3 * quarter]
        values = [load_merged(spot) for spot in spots]
        order_pair(values, 0, 2)
        order_pair(values, 1, 3)
        order_pair(values, 0, 1)
        order_pair(values, 2, 3)
        for spot, value in zip(spots, values):
            store(spot, value)
    for offset in range(0, total, quarter):
        clean_block(load_merged, store, offset, quarter)


def merge(back, owner, place):
    size = back.shape[0]
    local = back.shape[1] // LANES - 1
    return pl.pallas_call(
        merge_kernel,
        out_shape=(
            jax.ShapeDtypeStruct((local, KEEP), F32),
            jax.ShapeDtypeStruct(owner.shape, F32),
        ),
        scratch_shapes=[
            pltpu.VMEM((size * local, LANES), F32),
            pltpu.VMEM((LANES, size * local), F32),
            pltpu.VMEM((LANES, size * local), F32),
        ],
        compiler_params=pltpu.CompilerParams(vmem_limit_bytes=VMEM),
        name="merge",
    )(back, owner, place)


def exchange(x):
    return lax.all_to_all(x, "cand", split_axis=0, concat_axis=0, tiled=True)


def on_device(users, items, probes, gate_weight, gate_bias, cross_weight, cross_bias, out_weight,
              row_device, row_item, row_request):
    size = lax.axis_size("cand")
    local = users.shape[0]
    rows = row_item.shape[0]
    fetch = max(2, 2 * rows // size)
    own = users.reshape(1, local * EMB, D)
    queries = exchange(jnp.broadcast_to(own, (size, local * EMB, D)))
    queries = queries.reshape(size * local * EMB, D)
    owner = row_device.reshape(1, rows)
    codes, place, gate_full, bias_full = plan(
        owner, row_item.reshape(1, rows), row_request.reshape(1, rows), probes,
        gate_weight, gate_bias.reshape(1, PAIRS), size,
    )
    codes = exchange(codes)
    scores = score(queries, items, gate_full, bias_full)
    result = rank(
        scores, queries, items, codes, cross_weight, cross_bias, out_weight.reshape(1, -1),
        local, fetch,
    )
    top, rerank = merge(exchange(result), owner, place)
    return top, rerank.reshape(rows)


def solution(mesh):
    split_rows = P(("groups", "cand"), None)
    split = P(("groups", "cand"))
    return jax.shard_map(
        on_device,
        mesh=mesh,
        in_specs=(split_rows, split_rows, split_rows, P(), P(), P(), P(), P(), split_rows, split, split),
        out_specs=(split_rows, split),
        check_vma=False,
    )
```

```python
import functools
import math

import jax
import jax.numpy as jnp
from jax import lax
from jax.experimental import pallas as pl
from jax.experimental.pallas import tpu as pltpu
from jax.sharding import PartitionSpec as P

EMB = 8
D = 128
PAIRS = EMB * EMB
PROBES = 32
KEEP = 96
CL_DEV = 2
REQ_DEV = 4
LANES = 128
SUBLANES = 4
BLOCKS = 2
COLUMNS = 256
NEVER = -1e30
TILE_COLS = 256
GROUP = 4
BASE = 32
LOG2E = math.log2(math.e)
SCALE = 1.0 / math.sqrt(D)
VMEM = 56 * 1024 * 1024

F32 = jnp.float32
BF16 = jnp.bfloat16
NT = (((1,), (1,)), ((), ()))


def iota(shape, dim):
    return lax.broadcasted_iota(jnp.int32, shape, dim)


def dot(a, b):
    return jnp.dot(a, b, preferred_element_type=F32)


def dot_nt(a, b):
    return lax.dot_general(a, b, NT, preferred_element_type=F32)


def ones_where(cond):
    return jnp.where(cond, 1.0, 0.0).astype(BF16)


def message(row, size):
    return pl.ds(row, size, stride=SUBLANES)


def tree_sum(values):
    values = [(a + b).astype(F32) for a, b in zip(values[::2], values[1::2])]
    while len(values) > 1:
        values = [a + b for a, b in zip(values[::2], values[1::2])]
    return values[0]


def split_two(x):
    high = x.astype(BF16)
    return high, (x - high.astype(F32)).astype(BF16)


def plan_kernel(owner_ref, item_ref, request_ref, probes_ref, gate_ref, bias_ref,
                codes_ref, place_ref, gate_out, bias_out):
    rows = owner_ref.shape[1]
    size = codes_ref.shape[0] // SUBLANES
    at = owner_ref[...] == iota((size, rows), 0)
    at_one = ones_where(at)
    before = ones_where(iota((rows, rows), 0) < iota((rows, rows), 1))
    rank = dot(at_one, before)
    place = jnp.sum(jnp.where(at, rank, 0.0), axis=0, keepdims=True).astype(jnp.int32)
    place_ref[...] = place
    slots = ones_where(place == iota((LANES, rows), 0))
    item = item_ref[...]
    values = (item // BASE, item % BASE, request_ref[...])
    spread = jnp.concatenate(
        [jnp.where(at, value.astype(F32), 0.0).astype(BF16) for value in values], axis=0
    )
    codes = dot_nt(spread, slots)
    codes_ref[...] = jnp.zeros_like(codes_ref)
    items = (codes[:size] * BASE + codes[size : 2 * size]).astype(jnp.int32)
    codes_ref[message(0, size), :] = items
    codes_ref[message(1, size), :] = codes[2 * size :].astype(jnp.int32)
    requests, probes = probes_ref.shape
    lane = iota((size, LANES), 1)
    masks = jnp.zeros((size, LANES), F32)
    for cluster in range(CL_DEV):
        ids = iota((size, probes), 0) * CL_DEV + cluster
        for request in range(requests):
            hit = jnp.where(probes_ref[request : request + 1, :] == ids, 1.0, 0.0)
            any_hit = jnp.max(hit, axis=1, keepdims=True)
            masks = jnp.where(lane == cluster * requests + request, any_hit, masks)
    codes_ref[message(2, size), :] = masks.astype(jnp.int32)
    side = GROUP * PAIRS
    step = GROUP * EMB
    row, col = iota((side, PAIRS), 0), iota((side, PAIRS), 1)
    select = ones_where((row % EMB) * EMB + row // step == col)
    part = dot_nt(select, gate_ref[...]).astype(BF16)
    full = dot_nt(part, select)
    same = (iota((side, side), 0) // EMB) % GROUP == (iota((side, side), 1) // EMB) % GROUP
    gate_out[...] = jnp.where(same, full, 0.0).astype(BF16)
    order = (row % EMB) * EMB + row // step == col
    column = jnp.sum(jnp.where(order, bias_ref[...], 0.0), axis=1, keepdims=True)
    bias_out[...] = jnp.broadcast_to(column, bias_out.shape).astype(BF16)


def plan(owner, item, request, probes, gate_weight, gate_bias, size):
    rows = owner.shape[1]
    return pl.pallas_call(
        plan_kernel,
        out_shape=(
            jax.ShapeDtypeStruct((size * SUBLANES, LANES), jnp.int32),
            jax.ShapeDtypeStruct((1, rows), jnp.int32),
            jax.ShapeDtypeStruct((GROUP * PAIRS, GROUP * PAIRS), BF16),
            jax.ShapeDtypeStruct((GROUP * PAIRS, LANES), BF16),
        ),
        compiler_params=pltpu.CompilerParams(vmem_limit_bytes=VMEM),
        name="plan",
    )(owner, item, request, probes, gate_weight, gate_bias)


def score_kernel(query_ref, items_ref, gate_ref, bias_ref, scores_ref,
                 dots_a, dots_b, num_ref, den_ref, *logits):
    query_rows = query_ref.shape[0]
    tiles = items_ref.shape[0] // TILE_COLS
    step = GROUP * EMB
    groups = query_rows // step
    row_blocks = query_rows // TILE_COLS

    def piece(tile, index, out):
        j, block = index // row_blocks, index % row_blocks
        start = pl.multiple_of(block * TILE_COLS, TILE_COLS)
        lanes = pl.multiple_of(j * D, D)
        values = dot_nt(
            query_ref[pl.ds(start, TILE_COLS), :],
            items_ref[tile * TILE_COLS : (tile + 1) * TILE_COLS, pl.ds(lanes, D)],
        )
        out[j, pl.ds(start, TILE_COLS), :] = (values * SCALE).astype(BF16)

    def gate(dots, group, out):
        start = pl.multiple_of(group * step, step)
        part = dots[:, pl.ds(start, step), :].reshape(GROUP * PAIRS, TILE_COLS)
        out[...] = dot(gate_ref[...], part).astype(BF16)

    def mix(dots, group, logits):
        start = pl.multiple_of(group * step, step)
        weights, products = [], []
        for j in range(EMB):
            bias = bias_ref[j * step : (j + 1) * step, :]
            logit = logits[j * step : (j + 1) * step, :] + jnp.concatenate([bias, bias], axis=1)
            power = jnp.exp2(jnp.minimum(logit * LOG2E, 126.0))
            weight = jnp.maximum(jnp.log(1.0 + power), logit)
            weights.append(weight)
            products.append(weight * dots[j, pl.ds(start, step), :])
        den = tree_sum(weights)
        num = tree_sum(products)
        for half in range(TILE_COLS // LANES):
            lanes = slice(half * LANES, (half + 1) * LANES)
            num_ref[half, pl.ds(start, step), :] = num[:, lanes]
            den_ref[half, pl.ds(start, step), :] = den[:, lanes]

    buffers = (dots_a, dots_b)

    @pl.loop(0, groups)
    def _(index):
        piece(0, index, dots_a)

    for tile in range(tiles):
        dots, ahead = buffers[tile % 2], buffers[(tile + 1) % 2]
        gate(dots, 0, logits[0])
        gate(dots, 1, logits[1])

        @pl.loop(0, groups // 8)
        def _(quad):
            for phase in range(4):
                first = quad * 8 + phase * 2
                here, there = logits[2 * (phase % 2) : 2 * (phase % 2) + 2], logits[2 - 2 * (phase % 2) : 4 - 2 * (phase % 2)]
                if tile + 1 < tiles:
                    piece(tile + 1, first, ahead)
                    piece(tile + 1, first + 1, ahead)
                for k in range(2):
                    gate(dots, jnp.minimum(first + 2 + k, groups - 1), there[k])
                for k in range(2):
                    mix(dots, first + k, here[k])

        for half in range(TILE_COLS // LANES):
            num = jnp.zeros((query_rows // EMB, LANES), F32)
            den = jnp.ones((query_rows // EMB, LANES), F32)
            for i in range(EMB):
                num = num + num_ref[half, pl.ds(i, query_rows // EMB, stride=EMB), :]
                den = den + den_ref[half, pl.ds(i, query_rows // EMB, stride=EMB), :]
            start = tile * TILE_COLS + half * LANES
            scores_ref[start : start + LANES, :] = (num / den).T


def score(queries, items, gate_full, bias_full):
    query_rows, item_rows = queries.shape[0], items.shape[0]
    return pl.pallas_call(
        score_kernel,
        out_shape=jax.ShapeDtypeStruct((item_rows, query_rows // EMB), F32),
        scratch_shapes=[
            pltpu.VMEM((EMB, query_rows, TILE_COLS), BF16),
            pltpu.VMEM((EMB, query_rows, TILE_COLS), BF16),
            pltpu.VMEM((TILE_COLS // LANES, query_rows, LANES), F32),
            pltpu.VMEM((TILE_COLS // LANES, query_rows, LANES), F32),
        ]
        + [pltpu.VMEM((GROUP * PAIRS, TILE_COLS), BF16) for _ in range(4)],
        compiler_params=pltpu.CompilerParams(vmem_limit_bytes=VMEM),
        name="score",
    )(queries, items, gate_full, bias_full)


def batcher(count):
    pairs = []
    p = 1
    while p < count:
        k = p
        while k >= 1:
            for j in range(k % p, count - k, 2 * k):
                for i in range(min(k, count - j - k)):
                    if (i + j) // (2 * p) == (i + j + k) // (2 * p):
                        pairs.append((i + j, i + j + k))
            k //= 2
        p *= 2
    return pairs


def order_pair(values, i, j):
    values[i], values[j] = jnp.maximum(values[i], values[j]), jnp.minimum(values[i], values[j])


def clean(values):
    stride = len(values) // 2
    while stride:
        for i in range(len(values)):
            if not i & stride:
                order_pair(values, i, i + stride)
        stride //= 2


def clean_block(load, store, start, count):
    values = [load(start + i) for i in range(count)]
    clean(values)
    for i in range(count):
        store(start + i, values[i])


def sort_all(load, store, load_sorted, total, block):
    for start in range(0, total, block):
        values = [load(start + i) for i in range(block)]
        for i, j in batcher(block):
            order_pair(values, i, j)
        for i in range(block):
            store(start + i, values[i])
    size = 2 * block
    while size <= total:
        for start in range(0, total, size):
            if size == 2 * block:
                upper, lower = [], []
                for i in range(block):
                    a, b = load_sorted(start + i), load_sorted(start + size - 1 - i)
                    upper.append(jnp.maximum(a, b))
                    lower.append(jnp.minimum(a, b))
                for offset, values in ((0, upper), (block, lower[::-1])):
                    clean(values)
                    for i in range(block):
                        store(start + offset + i, values[i])
            else:
                half, quarter = size // 2, size // 4
                for i in range(quarter):
                    spots = (i, i + quarter, size - 1 - i - quarter, size - 1 - i)
                    values = [load_sorted(start + spot) for spot in spots]
                    order_pair(values, 0, 3)
                    order_pair(values, 1, 2)
                    order_pair(values, 0, 1)
                    order_pair(values, 2, 3)
                    for spot, value in zip(spots, values):
                        store(start + spot, value)
                for offset in range(0, size, quarter):
                    clean_block(load_sorted, store, start + offset, quarter)
        size *= 2


def merge_top(load, store, load_merged, partner, total):
    quarter = total // 4
    done = {}
    for i in range(quarter):
        spots = [i, i + quarter, i + 2 * quarter, i + 3 * quarter]
        values = [jnp.maximum(load(spot), partner(load(total - 1 - spot))) for spot in spots]
        order_pair(values, 0, 2)
        order_pair(values, 1, 3)
        order_pair(values, 0, 1)
        order_pair(values, 2, 3)
        for spot, value in zip(spots, values):
            store(spot, value)
    for offset in range(0, total, quarter):
        clean_block(load_merged, store, offset, quarter)


def rank_kernel(scores_ref, query_ref, codes_ref, items_hbm, weight_hbm, bias_ref, out_weight_ref,
                result_ref, weight_ref, table_ref, query_f32, pair_ref, sort_a, sort_b, best_ref,
                pick_ref, first_ref, state_ref, round_a, round_b, weight_sem, items_sem, *, fetch):
    item_rows, requests = scores_ref.shape
    weight_copy = pltpu.make_async_copy(weight_hbm, weight_ref, weight_sem)
    items_copy = pltpu.make_async_copy(items_hbm, table_ref.at[pl.ds(0, item_rows), :], items_sem)
    items_copy.start()
    weight_copy.start()
    size = codes_ref.shape[0] // SUBLANES
    local = requests // size

    query_f32[...] = query_ref[...].astype(F32)
    for i in range(EMB):
        users = query_f32[pl.ds(i, requests, stride=EMB), :].astype(BF16)
        table_ref[item_rows:, i * D : (i + 1) * D] = users
    pair_ref[:, :requests], pair_ref[:, requests:] = split_two(scores_ref[...])
    items_copy.wait()
    weight_copy.wait()
    best_of(scores_ref, codes_ref, result_ref, sort_a, sort_b, best_ref, local)

    total = size * fetch
    block = total // BLOCKS
    width = first_ref.shape[-1]
    code_item = codes_ref[message(0, size), :]
    digits = jnp.concatenate(
        [code_item // BASE, code_item % BASE, codes_ref[message(1, size), :]], axis=1
    ).astype(F32).astype(BF16)
    answer = jnp.zeros((size, LANES), F32)
    for part in range(BLOCKS):
        start = part * block
        pick, first, state = pick_ref.at[part], first_ref.at[part], state_ref.at[part]
        rounded = (round_a.at[part], round_b.at[part])

        def source_of(shape, dim):
            row = (iota(shape, dim) + start).astype(F32)
            return jnp.floor((row + 0.5) * (1.0 / fetch))

        from_source = ones_where(source_of((block, size), 0) == iota((block, size), 1).astype(F32))
        taken = dot(from_source, digits)
        slot = iota((block, LANES), 0) + start - source_of((block, LANES), 0).astype(jnp.int32) * fetch
        mine = slot == iota((block, LANES), 1)
        item = jnp.sum(
            jnp.where(mine, taken[:, :LANES] * BASE + taken[:, LANES : 2 * LANES], 0.0),
            axis=1, keepdims=True,
        ).astype(jnp.int32)
        request = jnp.sum(
            jnp.where(mine, taken[:, 2 * LANES :], 0.0), axis=1, keepdims=True
        ).astype(jnp.int32)
        asked = request == iota((block, requests), 1)
        pick[:, :item_rows] = ones_where(item == iota((block, item_rows), 1))
        pick[:, item_rows:] = ones_where(asked)
        mixed = dot(pick[:, :item_rows], pair_ref[...])
        mixed = jnp.where(asked, mixed[:, :requests] + mixed[:, requests:], 0.0)
        partial = mixed[:, :LANES]
        for i in range(1, requests // LANES):
            partial = partial + mixed[:, i * LANES : (i + 1) * LANES]

        for column in range(0, width, COLUMNS):
            columns = slice(column, column + COLUMNS)
            values = dot(pick[...], table_ref[:, columns])
            first[:, columns] = values
            rounded[0][:, columns] = values.astype(BF16)
        layers = weight_ref.shape[0]
        for layer in range(layers):
            for column in range(0, width, COLUMNS):
                columns = slice(column, column + COLUMNS)
                hidden = dot(rounded[layer % 2][...], weight_ref[layer, :, columns])
                hidden = hidden + bias_ref[layer : layer + 1, columns]
                before = (state if layer else first)[:, columns]
                after = first[:, columns] * hidden + before
                if layer + 1 < layers:
                    state[:, columns] = after
                    rounded[(layer + 1) % 2][:, columns] = after.astype(BF16)
                else:
                    weighted = after * out_weight_ref[:, columns]
                    for i in range(COLUMNS // LANES):
                        partial = partial + weighted[:, i * LANES : (i + 1) * LANES]
        column = jnp.sum(partial, axis=1, keepdims=True)
        placed = jnp.where(mine, column, 0.0)
        to_source = ones_where(source_of((size, block), 1) == iota((size, block), 0).astype(F32))
        high, rest = split_two(placed)
        middle, low = split_two(placed - high.astype(F32))
        answer = answer + (dot(to_source, high) + (dot(to_source, middle) + dot(to_source, low)))
    spare = LANES - KEEP
    free = iota(answer.shape, 1) >= KEEP
    for row in range(local):
        moved = pltpu.roll(answer, (KEEP - row * spare) % LANES, 1)
        result_ref[message(row, size), :] = jnp.where(free, moved, result_ref[message(row, size), :])


def best_of(scores_ref, codes_ref, result_ref, sort_a, sort_b, best_ref, local):
    size = codes_ref.shape[0] // SUBLANES
    item_rows, requests = scores_ref.shape
    lists = item_rows // EMB
    masks = codes_ref[message(2, size), :].astype(F32).astype(BF16)
    lane, from_row = iota((LANES, requests), 1), iota((LANES, requests), 0)
    source = iota((size, requests), 1) // local == iota((size, requests), 0)
    allowed = []
    for cluster in range(CL_DEV):
        spread = dot(masks, ones_where(from_row == cluster * local + lane % local))
        allowed.append(jnp.sum(jnp.where(source, spread, 0.0), axis=0, keepdims=True) > 0.5)
    for chunk in range(requests // LANES):
        lanes = slice(chunk * LANES, (chunk + 1) * LANES)
        fits = [jnp.broadcast_to(a[:, lanes], (EMB, LANES)) for a in allowed]

        def load(i):
            values = scores_ref[i * EMB : (i + 1) * EMB, lanes]
            return jnp.where(fits[i * CL_DEV // lists], values, NEVER)

        def reader(ref):
            return lambda i: ref[i]

        def writer(ref):
            def store(i, value):
                ref[i] = value
            return store

        sort_all(load, writer(sort_a), reader(sort_a), lists, 32)
        held, other = sort_a, sort_b
        shift = EMB // 2
        while shift:
            merge_top(
                reader(held), writer(other), reader(other),
                functools.partial(pltpu.roll, shift=shift, axis=0), lists,
            )
            held, other = other, held
            shift //= 2
        for i in range(lists):
            best_ref[i : i + 1, :] = held[i][:1, :]
        best_ref[...] = best_ref[...].T
        per_chunk = LANES // local
        for r in range(local):
            start = chunk * per_chunk * SUBLANES + r
            result_ref[pl.ds(start, per_chunk, stride=SUBLANES), :] = (
                best_ref[pl.ds(r, per_chunk, stride=local), :]
            )


def rank(scores, queries, items, codes, cross_weight, cross_bias, out_weight, fetch):
    requests = scores.shape[1]
    vmem = pl.BlockSpec(memory_space=pltpu.VMEM)
    item_rows, width = items.shape
    total = codes.shape[0] // SUBLANES * fetch
    block = (BLOCKS, total // BLOCKS)
    anywhere = pl.BlockSpec(memory_space=pl.ANY)
    return pl.pallas_call(
        functools.partial(rank_kernel, fetch=fetch),
        out_shape=jax.ShapeDtypeStruct(codes.shape, F32),
        in_specs=[vmem, vmem, vmem, anywhere, anywhere, vmem, vmem],
        out_specs=vmem,
        scratch_shapes=[
            pltpu.VMEM(cross_weight.shape, BF16),
            pltpu.VMEM((item_rows + requests, width), BF16),
            pltpu.VMEM(queries.shape, F32),
            pltpu.VMEM((item_rows, 2 * requests), BF16),
            pltpu.VMEM((item_rows // EMB, EMB, LANES), F32),
            pltpu.VMEM((item_rows // EMB, EMB, LANES), F32),
            pltpu.VMEM((LANES, LANES), F32),
            pltpu.VMEM((*block, item_rows + requests), BF16),
            pltpu.VMEM((*block, width), F32),
            pltpu.VMEM((*block, width), F32),
            pltpu.VMEM((*block, width), BF16),
            pltpu.VMEM((*block, width), BF16),
            pltpu.SemaphoreType.DMA,
            pltpu.SemaphoreType.DMA,
        ],
        compiler_params=pltpu.CompilerParams(vmem_limit_bytes=VMEM),
        name="rank",
    )(scores, queries, codes, items, cross_weight, cross_bias, out_weight)


def merge_kernel(back_ref, owner_ref, place_ref, top_ref, rerank_ref, list_ref, merge_a, merge_b):
    size = back_ref.shape[0] // SUBLANES
    local = top_ref.shape[0]
    rows = owner_ref.shape[1]
    at = owner_ref[...] == iota((size, rows), 0)
    spread = jnp.zeros((size, rows), F32)
    spare = LANES - KEEP
    for row in range(local):
        lane = iota((LANES, rows), 0)
        held = jnp.where(lane >= KEEP, lane - KEEP + row * spare, -1)
        slots = ones_where(place_ref[...] == held)
        answer = back_ref[message(row, size), :]
        high, rest = split_two(answer)
        middle, low = split_two(answer - high.astype(F32))
        spread = spread + (dot(high, slots) + (dot(middle, slots) + dot(low, slots)))
    rerank_ref[...] = jnp.sum(jnp.where(at, spread, 0.0), axis=0)

    for r in range(local):
        best = back_ref[message(r, size), :]
        list_ref[pl.ds(r, size, stride=local), :] = jnp.where(iota(best.shape, 1) < KEEP, best, NEVER)
    chunks = size * local // LANES
    merge_a[...] = list_ref[...].T

    def reader(ref, chunk=0):
        return lambda i: ref[i : i + 1, chunk * LANES : (chunk + 1) * LANES]

    def writer(ref):
        def store(i, value):
            ref[i : i + 1, :LANES] = value
        return store

    held, other = merge_a, merge_b
    while chunks > 1:
        half = chunks // 2
        for chunk in range(half):
            take = slice(chunk * LANES, (chunk + 1) * LANES)

            def load(i, ref=held, first=chunk, second=chunk + half):
                return ref[i : i + 1, first * LANES : (first + 1) * LANES]

            def store(i, value, ref=other, take=take):
                ref[i : i + 1, take] = value

            def read(i, ref=other, take=take):
                return ref[i : i + 1, take]

            merge_pairs(
                load,
                lambda i, ref=held, c=chunk + half: ref[i : i + 1, c * LANES : (c + 1) * LANES],
                store, read, LANES,
            )
        held, other = other, held
        chunks = half
    shift = LANES // 2
    while shift >= local:
        merge_top(
            reader(held), writer(other), reader(other),
            functools.partial(pltpu.roll, shift=LANES - shift, axis=1), LANES,
        )
        held, other = other, held
        shift //= 2
    top_ref[...] = held[:, :LANES].T[:local, :KEEP]


def merge_pairs(load, load_other, store, load_merged, total):
    for i in range(total):
        store(i, jnp.maximum(load(i), load_other(total - 1 - i)))
    quarter = total // 4
    for i in range(quarter):
        spots = [i, i + quarter, i + 2 * quarter, i + 3 * quarter]
        values = [load_merged(spot) for spot in spots]
        order_pair(values, 0, 2)
        order_pair(values, 1, 3)
        order_pair(values, 0, 1)
        order_pair(values, 2, 3)
        for spot, value in zip(spots, values):
            store(spot, value)
    for offset in range(0, total, quarter):
        clean_block(load_merged, store, offset, quarter)


def merge(back, owner, place, local):
    size = back.shape[0] // SUBLANES
    return pl.pallas_call(
        merge_kernel,
        out_shape=(
            jax.ShapeDtypeStruct((local, KEEP), F32),
            jax.ShapeDtypeStruct(owner.shape[1:], F32),
        ),
        scratch_shapes=[
            pltpu.VMEM((size * local, LANES), F32),
            pltpu.VMEM((LANES, size * local), F32),
            pltpu.VMEM((LANES, size * local), F32),
        ],
        compiler_params=pltpu.CompilerParams(vmem_limit_bytes=VMEM),
        name="merge",
    )(back, owner, place)


def exchange(x):
    return lax.all_to_all(x, "cand", split_axis=0, concat_axis=0, tiled=True)


def on_device(users, items, probes, gate_weight, gate_bias, cross_weight, cross_bias, out_weight,
              row_device, row_item, row_request):
    size = lax.axis_size("cand")
    local = users.shape[0]
    rows = row_item.shape[0]
    fetch = max(2, 2 * rows // size)
    own = users.reshape(1, local * EMB, D)
    queries = exchange(jnp.broadcast_to(own, (size, local * EMB, D)))
    queries = queries.reshape(size * local * EMB, D)
    owner = row_device.reshape(1, rows)
    codes, place, gate_full, bias_full = plan(
        owner, row_item.reshape(1, rows), row_request.reshape(1, rows), probes,
        gate_weight, gate_bias.reshape(1, PAIRS), size,
    )
    queries, codes = lax.optimization_barrier((queries, codes))
    codes = exchange(codes)
    scores = score(queries, items, gate_full, bias_full)
    result = rank(
        scores, queries, items, codes, cross_weight, cross_bias, out_weight.reshape(1, -1), fetch
    )
    return merge(exchange(result), owner, place, local)


def solution(mesh):
    split_rows = P(("groups", "cand"), None)
    split = P(("groups", "cand"))
    return jax.shard_map(
        on_device,
        mesh=mesh,
        in_specs=(split_rows, split_rows, split_rows, P(), P(), P(), P(), P(), split_rows, split, split),
        out_specs=(split_rows, split),
        check_vma=False,
    )
```

```python
import functools
import math

import jax
import jax.numpy as jnp
from jax import lax
from jax.experimental import pallas as pl
from jax.experimental.pallas import tpu as pltpu
from jax.sharding import PartitionSpec as P

EMB = 8
D = 128
PAIRS = EMB * EMB
PROBES = 32
KEEP = 96
CL_DEV = 2
REQ_DEV = 4
LANES = 128
SUBLANES = 4
BLOCKS = 2
SORT_AT = 0
COLUMNS = 256
NEVER = -1e30
TILE_COLS = 256
GROUP = 4
UNROLL = 32
AHEAD = 8
ROWS = 512
BASE = 32
LOG2E = math.log2(math.e)
SCALE = 1.0 / math.sqrt(D)
VMEM = 56 * 1024 * 1024

F32 = jnp.float32
BF16 = jnp.bfloat16
NT = (((1,), (1,)), ((), ()))


def iota(shape, dim):
    return lax.broadcasted_iota(jnp.int32, shape, dim)


def dot(a, b):
    return jnp.dot(a, b, preferred_element_type=F32)


def dot_nt(a, b):
    return lax.dot_general(a, b, NT, preferred_element_type=F32)


def ones_where(cond):
    return jnp.where(cond, 1.0, 0.0).astype(BF16)


def message(row, size):
    return pl.ds(row, size, stride=SUBLANES)


def tree_sum(values):
    values = [(a + b).astype(F32) for a, b in zip(values[::2], values[1::2])]
    while len(values) > 1:
        values = [a + b for a, b in zip(values[::2], values[1::2])]
    return values[0]


def split_two(x):
    high = x.astype(BF16)
    return high, (x - high.astype(F32)).astype(BF16)


def plan_kernel(owner_ref, item_ref, request_ref, probes_ref, gate_ref, bias_ref,
                codes_ref, place_ref, gate_out, bias_out):
    rows = owner_ref.shape[1]
    size = codes_ref.shape[0] // SUBLANES
    at = owner_ref[...] == iota((size, rows), 0)
    at_one = ones_where(at)
    before = ones_where(iota((rows, rows), 0) < iota((rows, rows), 1))
    rank = dot(at_one, before)
    place = jnp.sum(jnp.where(at, rank, 0.0), axis=0, keepdims=True).astype(jnp.int32)
    place_ref[...] = place
    slots = ones_where(place == iota((LANES, rows), 0))
    item = item_ref[...]
    values = (item // BASE, item % BASE, request_ref[...])
    spread = jnp.concatenate(
        [jnp.where(at, value.astype(F32), 0.0).astype(BF16) for value in values], axis=0
    )
    codes = dot_nt(spread, slots)
    codes_ref[...] = jnp.zeros_like(codes_ref)
    items = (codes[:size] * BASE + codes[size : 2 * size]).astype(jnp.int32)
    codes_ref[message(0, size), :] = items
    codes_ref[message(1, size), :] = codes[2 * size :].astype(jnp.int32)
    requests, probes = probes_ref.shape
    lane = iota((size, LANES), 1)
    masks = jnp.zeros((size, LANES), F32)
    for cluster in range(CL_DEV):
        ids = iota((size, probes), 0) * CL_DEV + cluster
        for request in range(requests):
            hit = jnp.where(probes_ref[request : request + 1, :] == ids, 1.0, 0.0)
            any_hit = jnp.max(hit, axis=1, keepdims=True)
            masks = jnp.where(lane == cluster * requests + request, any_hit, masks)
    codes_ref[message(2, size), :] = masks.astype(jnp.int32)
    side = GROUP * PAIRS
    step = GROUP * EMB
    row, col = iota((side, PAIRS), 0), iota((side, PAIRS), 1)
    select = ones_where((row % step // GROUP) * EMB + row // step == col)
    part = dot_nt(select, gate_ref[...]).astype(BF16)
    full = dot_nt(part, select)
    same = iota((side, side), 0) % GROUP == iota((side, side), 1) % GROUP
    gate_out[...] = jnp.where(same, full, 0.0).astype(BF16)
    order = (row % step // GROUP) * EMB + row // step == col
    column = jnp.sum(jnp.where(order, bias_ref[...], 0.0), axis=1, keepdims=True)
    bias_out[...] = jnp.broadcast_to(column, bias_out.shape).astype(BF16)


def plan(owner, item, request, probes, gate_weight, gate_bias, size):
    rows = owner.shape[1]
    return pl.pallas_call(
        plan_kernel,
        out_shape=(
            jax.ShapeDtypeStruct((size * SUBLANES, LANES), jnp.int32),
            jax.ShapeDtypeStruct((1, rows), jnp.int32),
            jax.ShapeDtypeStruct((GROUP * PAIRS, GROUP * PAIRS), BF16),
            jax.ShapeDtypeStruct((GROUP * PAIRS, LANES), BF16),
        ),
        compiler_params=pltpu.CompilerParams(vmem_limit_bytes=VMEM),
        name="plan",
    )(owner, item, request, probes, gate_weight, gate_bias)


def score_kernel(query_ref, items_ref, gate_ref, bias_ref, scores_ref,
                 dots_ref, num_ref, den_ref, *logits):
    query_rows = query_ref.shape[0]
    tiles = items_ref.shape[0] // TILE_COLS
    step = GROUP * EMB
    groups = query_rows // step
    units = tiles * groups

    @pl.loop(0, tiles * EMB // AHEAD)
    def _(index):
        for k in range(AHEAD):
            piece = index * AHEAD + k
            tile, j = piece // EMB, piece % EMB
            start = pl.multiple_of(tile * TILE_COLS, TILE_COLS)
            lanes = pl.multiple_of(j * D, D)
            for block in range(query_rows // ROWS):
                rows = slice(block * ROWS, (block + 1) * ROWS)
                values = dot_nt(
                    query_ref[rows, :], items_ref[pl.ds(start, TILE_COLS), pl.ds(lanes, D)]
                )
                dots_ref[tile, j, rows, :] = (values * SCALE).astype(BF16)

    def place(unit):
        unit = jnp.minimum(unit, units - 1)
        tile, group = unit // groups, unit % groups
        return tile, pl.multiple_of(group * step, step), group

    def gate(unit, out):
        tile, start, _ = place(unit)
        part = dots_ref[tile, :, pl.ds(start, step), :].reshape(GROUP * PAIRS, TILE_COLS)
        out[...] = dot(gate_ref[...], part).astype(BF16)

    def mix(unit, logits):
        tile, start, _ = place(unit)
        weights, products = [], []
        for j in range(EMB):
            bias = bias_ref[j * step : (j + 1) * step, :]
            logit = logits[j * step : (j + 1) * step, :] + jnp.concatenate([bias, bias], axis=1)
            power = jnp.exp2(jnp.minimum(logit * LOG2E, 126.0))
            weight = jnp.maximum(jnp.log(1.0 + power), logit)
            weights.append(weight)
            products.append(weight * dots_ref[tile, j, pl.ds(start, step), :])
        totals = []
        for values in (weights, products):
            both = jnp.sum(tree_sum(values).reshape(step // (2 * GROUP), 2 * GROUP, TILE_COLS), axis=0)
            totals.append(both + pltpu.roll(both, GROUP, 0))
        return totals

    def keep(unit, even, odd):
        tile, _, group = place(unit)
        rows = pl.ds(pl.multiple_of(group * GROUP, 2 * GROUP), 2 * GROUP)
        upper = iota((2 * GROUP, TILE_COLS), 0) < GROUP
        for out, a, b in zip((den_ref, num_ref), even, odd):
            out[tile, rows, :] = jnp.where(upper, a, b)

    gate(0, logits[0])
    gate(1, logits[1])

    @pl.loop(0, units // UNROLL)
    def _(index):
        for phase in range(UNROLL // 2):
            first = index * UNROLL + phase * 2
            side = 2 * (phase % 2)
            here, there = logits[side : side + 2], logits[2 - side : 4 - side]
            for k in range(2):
                gate(first + 2 + k, there[k])
            keep(first, mix(first, here[0]), mix(first + 1, here[1]))

    for tile in range(tiles):
        values = num_ref[tile] / (1.0 + den_ref[tile])
        scores_ref[tile * TILE_COLS : (tile + 1) * TILE_COLS, :] = values.T


def score(queries, items, gate_full, bias_full):
    query_rows, item_rows = queries.shape[0], items.shape[0]
    tiles = item_rows // TILE_COLS
    return pl.pallas_call(
        score_kernel,
        out_shape=jax.ShapeDtypeStruct((item_rows, query_rows // EMB), F32),
        scratch_shapes=[
            pltpu.VMEM((tiles, EMB, query_rows, TILE_COLS), BF16),
            pltpu.VMEM((tiles, query_rows // EMB, TILE_COLS), F32),
            pltpu.VMEM((tiles, query_rows // EMB, TILE_COLS), F32),
        ]
        + [pltpu.VMEM((GROUP * PAIRS, TILE_COLS), BF16) for _ in range(4)],
        compiler_params=pltpu.CompilerParams(vmem_limit_bytes=VMEM),
        name="score",
    )(queries, items, gate_full, bias_full)


def batcher(count):
    pairs = []
    p = 1
    while p < count:
        k = p
        while k >= 1:
            for j in range(k % p, count - k, 2 * k):
                for i in range(min(k, count - j - k)):
                    if (i + j) // (2 * p) == (i + j + k) // (2 * p):
                        pairs.append((i + j, i + j + k))
            k //= 2
        p *= 2
    return pairs


def order_pair(values, i, j):
    values[i], values[j] = jnp.maximum(values[i], values[j]), jnp.minimum(values[i], values[j])


def clean(values):
    stride = len(values) // 2
    while stride:
        for i in range(len(values)):
            if not i & stride:
                order_pair(values, i, i + stride)
        stride //= 2


def clean_block(load, store, start, count):
    values = [load(start + i) for i in range(count)]
    clean(values)
    for i in range(count):
        store(start + i, values[i])


def sort_all(load, store, load_sorted, total, block):
    for start in range(0, total, block):
        values = [load(start + i) for i in range(block)]
        for i, j in batcher(block):
            order_pair(values, i, j)
        for i in range(block):
            store(start + i, values[i])
    size = 2 * block
    while size <= total:
        for start in range(0, total, size):
            if size == 2 * block:
                upper, lower = [], []
                for i in range(block):
                    a, b = load_sorted(start + i), load_sorted(start + size - 1 - i)
                    upper.append(jnp.maximum(a, b))
                    lower.append(jnp.minimum(a, b))
                for offset, values in ((0, upper), (block, lower[::-1])):
                    clean(values)
                    for i in range(block):
                        store(start + offset + i, values[i])
            else:
                half, quarter = size // 2, size // 4
                for i in range(quarter):
                    spots = (i, i + quarter, size - 1 - i - quarter, size - 1 - i)
                    values = [load_sorted(start + spot) for spot in spots]
                    order_pair(values, 0, 3)
                    order_pair(values, 1, 2)
                    order_pair(values, 0, 1)
                    order_pair(values, 2, 3)
                    for spot, value in zip(spots, values):
                        store(start + spot, value)
                for offset in range(0, size, quarter):
                    clean_block(load_sorted, store, start + offset, quarter)
        size *= 2


def merge_top(load, store, load_merged, partner, total):
    quarter = total // 4
    done = {}
    for i in range(quarter):
        spots = [i, i + quarter, i + 2 * quarter, i + 3 * quarter]
        values = [jnp.maximum(load(spot), partner(load(total - 1 - spot))) for spot in spots]
        order_pair(values, 0, 2)
        order_pair(values, 1, 3)
        order_pair(values, 0, 1)
        order_pair(values, 2, 3)
        for spot, value in zip(spots, values):
            store(spot, value)
    for offset in range(0, total, quarter):
        clean_block(load_merged, store, offset, quarter)


def rank_kernel(scores_ref, query_ref, codes_ref, items_hbm, weight_hbm, bias_ref, out_weight_ref,
                result_ref, weight_ref, table_ref, query_f32, user_f32, pair_ref, sort_a, sort_b, best_ref,
                pick_ref, first_ref, state_ref, round_a, round_b, weight_sem, items_sem, *, fetch):
    item_rows, requests = scores_ref.shape
    weight_copy = pltpu.make_async_copy(weight_hbm, weight_ref, weight_sem)
    items_copy = pltpu.make_async_copy(items_hbm, table_ref.at[pl.ds(0, item_rows), :], items_sem)
    items_copy.start()
    weight_copy.start()
    size = codes_ref.shape[0] // SUBLANES
    local = requests // size

    query_f32[...] = query_ref[...].astype(F32)
    for i in range(EMB):
        for r in range(local):
            rows = query_f32[pl.ds(i * local + r, size, stride=local * EMB), :]
            user_f32[i, pl.ds(r, size, stride=local), :] = rows
        table_ref[item_rows:, i * D : (i + 1) * D] = user_f32[i].astype(BF16)
    pair_ref[:, :requests], pair_ref[:, requests:] = split_two(scores_ref[...])
    items_copy.wait()
    weight_copy.wait()
    total = size * fetch
    block = total // BLOCKS
    width = first_ref.shape[-1]
    code_item = codes_ref[message(0, size), :]
    digits = jnp.concatenate(
        [code_item // BASE, code_item % BASE, codes_ref[message(1, size), :]], axis=1
    ).astype(F32).astype(BF16)
    answer = jnp.zeros((size, LANES), F32)

    def source_of(shape, dim, start):
        row = (iota(shape, dim) + start).astype(F32)
        return jnp.floor((row + 0.5) * (1.0 / fetch))

    def slot_of(start):
        source = source_of((block, LANES), 0, start).astype(jnp.int32)
        return iota((block, LANES), 0) + start - source * fetch == iota((block, LANES), 1)

    for part in range(BLOCKS):
        start = part * block
        pick = pick_ref.at[part]
        from_source = source_of((block, size), 0, start) == iota((block, size), 1).astype(F32)
        taken = dot(ones_where(from_source), digits)
        mine = slot_of(start)
        item = jnp.sum(
            jnp.where(mine, taken[:, :LANES] * BASE + taken[:, LANES : 2 * LANES], 0.0),
            axis=1, keepdims=True,
        ).astype(jnp.int32)
        request = jnp.sum(
            jnp.where(mine, taken[:, 2 * LANES :], 0.0), axis=1, keepdims=True
        ).astype(jnp.int32)
        pick[:, :item_rows] = ones_where(item == iota((block, item_rows), 1))
        pick[:, item_rows:] = ones_where(request == iota((block, requests), 1))

    layers = weight_ref.shape[0]
    for part in range(BLOCKS):
        for column in range(0, width, COLUMNS):
            columns = slice(column, column + COLUMNS)
            values = dot(pick_ref[part], table_ref[:, columns])
            first_ref[part, :, columns] = values
            round_a[part, :, columns] = values.astype(BF16)
    partial = [None] * BLOCKS
    rounded = (round_a, round_b)
    for layer in range(layers):
        for part in range(BLOCKS):
            for column in range(0, width, COLUMNS):
                columns = slice(column, column + COLUMNS)
                hidden = dot(rounded[layer % 2][part], weight_ref[layer, :, columns])
                hidden = hidden + bias_ref[layer : layer + 1, columns]
                first = first_ref[part, :, columns]
                after = first * hidden + (state_ref[part, :, columns] if layer else first)
                if layer + 1 < layers:
                    state_ref[part, :, columns] = after
                    rounded[(layer + 1) % 2][part, :, columns] = after.astype(BF16)
                else:
                    weighted = after * out_weight_ref[:, columns]
                    for i in range(COLUMNS // LANES):
                        term = weighted[:, i * LANES : (i + 1) * LANES]
                        partial[part] = term if partial[part] is None else partial[part] + term
        if layer == SORT_AT:
            best_of(scores_ref, codes_ref, result_ref, sort_a, sort_b, best_ref, local)
    for part in range(BLOCKS):
        start = part * block
        mixed = dot(pick_ref[part, :, :item_rows], pair_ref[...])
        mixed = mixed[:, :requests] + mixed[:, requests:]
        mixed = mixed * pick_ref[part, :, item_rows:].astype(F32)
        total_row = partial[part]
        for i in range(requests // LANES):
            total_row = total_row + mixed[:, i * LANES : (i + 1) * LANES]
        column = jnp.sum(total_row, axis=1, keepdims=True)
        placed = jnp.where(slot_of(start), column, 0.0)
        to_source = ones_where(
            source_of((size, block), 1, start) == iota((size, block), 0).astype(F32)
        )
        high, rest = split_two(placed)
        middle, low = split_two(placed - high.astype(F32))
        answer = answer + (dot(to_source, high) + (dot(to_source, middle) + dot(to_source, low)))
    spare = LANES - KEEP
    free = iota(answer.shape, 1) >= KEEP
    for row in range(local):
        moved = pltpu.roll(answer, (KEEP - row * spare) % LANES, 1)
        result_ref[message(row, size), :] = jnp.where(free, moved, result_ref[message(row, size), :])


def best_of(scores_ref, codes_ref, result_ref, sort_a, sort_b, best_ref, local):
    size = codes_ref.shape[0] // SUBLANES
    item_rows, requests = scores_ref.shape
    lists = item_rows // EMB
    masks = codes_ref[message(2, size), :].astype(F32).astype(BF16)
    lane, from_row = iota((LANES, requests), 1), iota((LANES, requests), 0)
    source = iota((size, requests), 1) // local == iota((size, requests), 0)
    allowed = []
    for cluster in range(CL_DEV):
        spread = dot(masks, ones_where(from_row == cluster * local + lane % local))
        allowed.append(jnp.sum(jnp.where(source, spread, 0.0), axis=0, keepdims=True) > 0.5)
    for chunk in range(requests // LANES):
        lanes = slice(chunk * LANES, (chunk + 1) * LANES)
        fits = [jnp.broadcast_to(a[:, lanes], (EMB, LANES)) for a in allowed]

        def load(i):
            values = scores_ref[i * EMB : (i + 1) * EMB, lanes]
            return jnp.where(fits[i * CL_DEV // lists], values, NEVER)

        def reader(ref):
            return lambda i: ref[i]

        def writer(ref):
            def store(i, value):
                ref[i] = value
            return store

        sort_all(load, writer(sort_a), reader(sort_a), lists, 32)
        held, other = sort_a, sort_b
        shift = EMB // 2
        while shift:
            merge_top(
                reader(held), writer(other), reader(other),
                functools.partial(pltpu.roll, shift=shift, axis=0), lists,
            )
            held, other = other, held
            shift //= 2
        for i in range(lists):
            best_ref[i : i + 1, :] = held[i][:1, :]
        best_ref[...] = best_ref[...].T
        per_chunk = LANES // local
        for r in range(local):
            start = chunk * per_chunk * SUBLANES + r
            result_ref[pl.ds(start, per_chunk, stride=SUBLANES), :] = (
                best_ref[pl.ds(r, per_chunk, stride=local), :]
            )


def rank(scores, queries, items, codes, cross_weight, cross_bias, out_weight, fetch):
    requests = scores.shape[1]
    vmem = pl.BlockSpec(memory_space=pltpu.VMEM)
    item_rows, width = items.shape
    total = codes.shape[0] // SUBLANES * fetch
    block = (BLOCKS, total // BLOCKS)
    anywhere = pl.BlockSpec(memory_space=pl.ANY)
    return pl.pallas_call(
        functools.partial(rank_kernel, fetch=fetch),
        out_shape=jax.ShapeDtypeStruct(codes.shape, F32),
        in_specs=[vmem, vmem, vmem, anywhere, anywhere, vmem, vmem],
        out_specs=vmem,
        scratch_shapes=[
            pltpu.VMEM(cross_weight.shape, BF16),
            pltpu.VMEM((item_rows + requests, width), BF16),
            pltpu.VMEM(queries.shape, F32),
            pltpu.VMEM((EMB, requests, D), F32),
            pltpu.VMEM((item_rows, 2 * requests), BF16),
            pltpu.VMEM((item_rows // EMB, EMB, LANES), F32),
            pltpu.VMEM((item_rows // EMB, EMB, LANES), F32),
            pltpu.VMEM((LANES, LANES), F32),
            pltpu.VMEM((*block, item_rows + requests), BF16),
            pltpu.VMEM((*block, width), F32),
            pltpu.VMEM((*block, width), F32),
            pltpu.VMEM((*block, width), BF16),
            pltpu.VMEM((*block, width), BF16),
            pltpu.SemaphoreType.DMA,
            pltpu.SemaphoreType.DMA,
        ],
        compiler_params=pltpu.CompilerParams(vmem_limit_bytes=VMEM),
        name="rank",
    )(scores, queries, codes, items, cross_weight, cross_bias, out_weight)


def merge_kernel(back_ref, owner_ref, place_ref, top_ref, rerank_ref, list_ref, merge_a, merge_b):
    size = back_ref.shape[0] // SUBLANES
    local = top_ref.shape[0]
    rows = owner_ref.shape[1]
    at = owner_ref[...] == iota((size, rows), 0)
    spread = jnp.zeros((size, rows), F32)
    spare = LANES - KEEP
    for row in range(local):
        lane = iota((LANES, rows), 0)
        held = jnp.where(lane >= KEEP, lane - KEEP + row * spare, -1)
        slots = ones_where(place_ref[...] == held)
        answer = back_ref[message(row, size), :]
        high, rest = split_two(answer)
        middle, low = split_two(answer - high.astype(F32))
        spread = spread + (dot(high, slots) + (dot(middle, slots) + dot(low, slots)))
    rerank_ref[...] = jnp.sum(jnp.where(at, spread, 0.0), axis=0)

    for r in range(local):
        best = back_ref[message(r, size), :]
        list_ref[pl.ds(r, size, stride=local), :] = jnp.where(iota(best.shape, 1) < KEEP, best, NEVER)
    chunks = size * local // LANES
    merge_a[...] = list_ref[...].T

    def reader(ref, chunk=0):
        return lambda i: ref[i : i + 1, chunk * LANES : (chunk + 1) * LANES]

    def writer(ref):
        def store(i, value):
            ref[i : i + 1, :LANES] = value
        return store

    held, other = merge_a, merge_b
    while chunks > 1:
        half = chunks // 2
        for chunk in range(half):
            take = slice(chunk * LANES, (chunk + 1) * LANES)

            def load(i, ref=held, first=chunk, second=chunk + half):
                return ref[i : i + 1, first * LANES : (first + 1) * LANES]

            def store(i, value, ref=other, take=take):
                ref[i : i + 1, take] = value

            def read(i, ref=other, take=take):
                return ref[i : i + 1, take]

            merge_pairs(
                load,
                lambda i, ref=held, c=chunk + half: ref[i : i + 1, c * LANES : (c + 1) * LANES],
                store, read, LANES,
            )
        held, other = other, held
        chunks = half
    shift = LANES // 2
    while shift >= local:
        merge_top(
            reader(held), writer(other), reader(other),
            functools.partial(pltpu.roll, shift=LANES - shift, axis=1), LANES,
        )
        held, other = other, held
        shift //= 2
    top_ref[...] = held[:, :LANES].T[:local, :KEEP]


def merge_pairs(load, load_other, store, load_merged, total):
    for i in range(total):
        store(i, jnp.maximum(load(i), load_other(total - 1 - i)))
    quarter = total // 4
    for i in range(quarter):
        spots = [i, i + quarter, i + 2 * quarter, i + 3 * quarter]
        values = [load_merged(spot) for spot in spots]
        order_pair(values, 0, 2)
        order_pair(values, 1, 3)
        order_pair(values, 0, 1)
        order_pair(values, 2, 3)
        for spot, value in zip(spots, values):
            store(spot, value)
    for offset in range(0, total, quarter):
        clean_block(load_merged, store, offset, quarter)


def merge(back, owner, place, local):
    size = back.shape[0] // SUBLANES
    return pl.pallas_call(
        merge_kernel,
        out_shape=(
            jax.ShapeDtypeStruct((local, KEEP), F32),
            jax.ShapeDtypeStruct(owner.shape[1:], F32),
        ),
        scratch_shapes=[
            pltpu.VMEM((size * local, LANES), F32),
            pltpu.VMEM((LANES, size * local), F32),
            pltpu.VMEM((LANES, size * local), F32),
        ],
        compiler_params=pltpu.CompilerParams(vmem_limit_bytes=VMEM),
        name="merge",
    )(back, owner, place)


def exchange(x):
    return lax.all_to_all(x, "cand", split_axis=0, concat_axis=0, tiled=True)


def on_device(users, items, probes, gate_weight, gate_bias, cross_weight, cross_bias, out_weight,
              row_device, row_item, row_request):
    size = lax.axis_size("cand")
    local = users.shape[0]
    rows = row_item.shape[0]
    fetch = max(2, 2 * rows // size)
    own = users.reshape(local, EMB, D).swapaxes(0, 1).reshape(1, local * EMB, D)
    queries = exchange(jnp.broadcast_to(own, (size, local * EMB, D)))
    queries = queries.reshape(size * local * EMB, D)
    owner = row_device.reshape(1, rows)
    codes, place, gate_full, bias_full = plan(
        owner, row_item.reshape(1, rows), row_request.reshape(1, rows), probes,
        gate_weight, gate_bias.reshape(1, PAIRS), size,
    )
    queries, codes = lax.optimization_barrier((queries, codes))
    codes = exchange(codes)
    scores = score(queries, items, gate_full, bias_full)
    result = rank(
        scores, queries, items, codes, cross_weight, cross_bias, out_weight.reshape(1, -1), fetch
    )
    return merge(exchange(result), owner, place, local)


def solution(mesh):
    split_rows = P(("groups", "cand"), None)
    split = P(("groups", "cand"))
    return jax.shard_map(
        on_device,
        mesh=mesh,
        in_specs=(split_rows, split_rows, split_rows, P(), P(), P(), P(), P(), split_rows, split, split),
        out_specs=(split_rows, split),
        check_vma=False,
    )
```

```python
import functools
import math

import jax
import jax.numpy as jnp
from jax import lax
from jax.experimental import pallas as pl
from jax.experimental.pallas import tpu as pltpu
from jax.sharding import PartitionSpec as P

EMB = 8
D = 128
PAIRS = EMB * EMB
PROBES = 32
KEEP = 96
CL_DEV = 2
REQ_DEV = 4
LANES = 128
SUBLANES = 4
BLOCKS = 2
SORT_AT = 0
COLUMNS = 256
NEVER = -1e30
TILE_COLS = 256
GROUP = 4
UNROLL = 32
AHEAD = 8
ROWS = 512
BASE = 32
LOG2E = math.log2(math.e)
SCALE = 1.0 / math.sqrt(D)
VMEM = 56 * 1024 * 1024

F32 = jnp.float32
BF16 = jnp.bfloat16
NT = (((1,), (1,)), ((), ()))


def iota(shape, dim):
    return lax.broadcasted_iota(jnp.int32, shape, dim)


def dot(a, b):
    return jnp.dot(a, b, preferred_element_type=F32)


def dot_nt(a, b):
    return lax.dot_general(a, b, NT, preferred_element_type=F32)


def ones_where(cond):
    return jnp.where(cond, 1.0, 0.0).astype(BF16)


def message(row, size):
    return pl.ds(row, size, stride=SUBLANES)


def tree_sum(values):
    values = [(a + b).astype(F32) for a, b in zip(values[::2], values[1::2])]
    while len(values) > 1:
        values = [a + b for a, b in zip(values[::2], values[1::2])]
    return values[0]


def split_two(x):
    high = x.astype(BF16)
    return high, (x - high.astype(F32)).astype(BF16)


def plan_kernel(owner_ref, item_ref, request_ref, probes_ref, gate_ref, bias_ref,
                codes_ref, place_ref, gate_out, bias_out):
    rows = owner_ref.shape[1]
    size = codes_ref.shape[0] // SUBLANES
    at = owner_ref[...] == iota((size, rows), 0)
    at_one = ones_where(at)
    before = ones_where(iota((rows, rows), 0) < iota((rows, rows), 1))
    rank = dot(at_one, before)
    place = jnp.sum(jnp.where(at, rank, 0.0), axis=0, keepdims=True).astype(jnp.int32)
    place_ref[...] = place
    slots = ones_where(place == iota((LANES, rows), 0))
    item = item_ref[...]
    values = (item // BASE, item % BASE, request_ref[...])
    spread = jnp.concatenate(
        [jnp.where(at, value.astype(F32), 0.0).astype(BF16) for value in values], axis=0
    )
    codes = dot_nt(spread, slots)
    codes_ref[...] = jnp.zeros_like(codes_ref)
    items = (codes[:size] * BASE + codes[size : 2 * size]).astype(jnp.int32)
    codes_ref[message(0, size), :] = items
    codes_ref[message(1, size), :] = codes[2 * size :].astype(jnp.int32)
    requests, probes = probes_ref.shape
    lane = iota((size, LANES), 1)
    masks = jnp.zeros((size, LANES), F32)
    for cluster in range(CL_DEV):
        ids = iota((size, probes), 0) * CL_DEV + cluster
        for request in range(requests):
            hit = jnp.where(probes_ref[request : request + 1, :] == ids, 1.0, 0.0)
            any_hit = jnp.max(hit, axis=1, keepdims=True)
            masks = jnp.where(lane == cluster * requests + request, any_hit, masks)
    codes_ref[message(2, size), :] = masks.astype(jnp.int32)
    side = GROUP * PAIRS
    step = GROUP * EMB
    row, col = iota((side, PAIRS), 0), iota((side, PAIRS), 1)
    select = ones_where((row % step // GROUP) * EMB + row // step == col)
    part = dot_nt(select, gate_ref[...]).astype(BF16)
    full = dot_nt(part, select)
    same = iota((side, side), 0) % GROUP == iota((side, side), 1) % GROUP
    gate_out[...] = jnp.where(same, full, 0.0).astype(BF16)
    order = (row % step // GROUP) * EMB + row // step == col
    column = jnp.sum(jnp.where(order, bias_ref[...], 0.0), axis=1, keepdims=True)
    bias_out[...] = jnp.broadcast_to(column, bias_out.shape).astype(BF16)


def plan(owner, item, request, probes, gate_weight, gate_bias, size):
    rows = owner.shape[1]
    return pl.pallas_call(
        plan_kernel,
        out_shape=(
            jax.ShapeDtypeStruct((size * SUBLANES, LANES), jnp.int32),
            jax.ShapeDtypeStruct((1, rows), jnp.int32),
            jax.ShapeDtypeStruct((GROUP * PAIRS, GROUP * PAIRS), BF16),
            jax.ShapeDtypeStruct((GROUP * PAIRS, LANES), BF16),
        ),
        compiler_params=pltpu.CompilerParams(vmem_limit_bytes=VMEM),
        name="plan",
    )(owner, item, request, probes, gate_weight, gate_bias)


def score_kernel(query_ref, items_ref, gate_ref, bias_ref, scores_ref,
                 dots_ref, num_ref, den_ref, *logits):
    query_rows = query_ref.shape[0]
    tiles = items_ref.shape[0] // TILE_COLS
    step = GROUP * EMB
    groups = query_rows // step
    units = tiles * groups

    @pl.loop(0, tiles * EMB // AHEAD)
    def _(index):
        for k in range(AHEAD):
            piece = index * AHEAD + k
            tile, j = piece // EMB, piece % EMB
            start = pl.multiple_of(tile * TILE_COLS, TILE_COLS)
            lanes = pl.multiple_of(j * D, D)
            for block in range(query_rows // ROWS):
                rows = slice(block * ROWS, (block + 1) * ROWS)
                values = dot_nt(
                    query_ref[rows, :], items_ref[pl.ds(start, TILE_COLS), pl.ds(lanes, D)]
                )
                dots_ref[tile, j, rows, :] = (values * SCALE).astype(BF16)

    def place(unit):
        unit = jnp.minimum(unit, units - 1)
        tile, group = unit // groups, unit % groups
        return tile, pl.multiple_of(group * step, step), group

    def gate(unit, out):
        tile, start, _ = place(unit)
        part = dots_ref[tile, :, pl.ds(start, step), :].reshape(GROUP * PAIRS, TILE_COLS)
        out[...] = dot(gate_ref[...], part).astype(BF16)

    def mix(unit, logits):
        tile, start, _ = place(unit)
        weights, products = [], []
        for j in range(EMB):
            bias = bias_ref[j * step : (j + 1) * step, :]
            logit = logits[j * step : (j + 1) * step, :] + jnp.concatenate([bias, bias], axis=1)
            power = jnp.exp2(jnp.minimum(logit * LOG2E, 126.0))
            weight = jnp.maximum(jnp.log(1.0 + power), logit)
            weights.append(weight)
            products.append(weight * dots_ref[tile, j, pl.ds(start, step), :])
        totals = []
        for values in (weights, products):
            both = jnp.sum(tree_sum(values).reshape(step // (2 * GROUP), 2 * GROUP, TILE_COLS), axis=0)
            totals.append(both + pltpu.roll(both, GROUP, 0))
        return totals

    def keep(unit, even, odd):
        tile, _, group = place(unit)
        rows = pl.ds(pl.multiple_of(group * GROUP, 2 * GROUP), 2 * GROUP)
        upper = iota((2 * GROUP, TILE_COLS), 0) < GROUP
        for out, a, b in zip((den_ref, num_ref), even, odd):
            out[tile, rows, :] = jnp.where(upper, a, b)

    gate(0, logits[0])
    gate(1, logits[1])

    @pl.loop(0, units // UNROLL)
    def _(index):
        for phase in range(UNROLL // 2):
            first = index * UNROLL + phase * 2
            side = 2 * (phase % 2)
            here, there = logits[side : side + 2], logits[2 - side : 4 - side]
            for k in range(2):
                gate(first + 2 + k, there[k])
            keep(first, mix(first, here[0]), mix(first + 1, here[1]))

    for tile in range(tiles):
        values = num_ref[tile] / (1.0 + den_ref[tile])
        scores_ref[tile * TILE_COLS : (tile + 1) * TILE_COLS, :] = values.T


def score(queries, items, gate_full, bias_full):
    query_rows, item_rows = queries.shape[0], items.shape[0]
    tiles = item_rows // TILE_COLS
    return pl.pallas_call(
        score_kernel,
        out_shape=jax.ShapeDtypeStruct((item_rows, query_rows // EMB), F32),
        scratch_shapes=[
            pltpu.VMEM((tiles, EMB, query_rows, TILE_COLS), BF16),
            pltpu.VMEM((tiles, query_rows // EMB, TILE_COLS), F32),
            pltpu.VMEM((tiles, query_rows // EMB, TILE_COLS), F32),
        ]
        + [pltpu.VMEM((GROUP * PAIRS, TILE_COLS), BF16) for _ in range(4)],
        compiler_params=pltpu.CompilerParams(vmem_limit_bytes=VMEM),
        name="score",
    )(queries, items, gate_full, bias_full)


def batcher(count):
    pairs = []
    p = 1
    while p < count:
        k = p
        while k >= 1:
            for j in range(k % p, count - k, 2 * k):
                for i in range(min(k, count - j - k)):
                    if (i + j) // (2 * p) == (i + j + k) // (2 * p):
                        pairs.append((i + j, i + j + k))
            k //= 2
        p *= 2
    return pairs


def order_pair(values, i, j):
    values[i], values[j] = jnp.maximum(values[i], values[j]), jnp.minimum(values[i], values[j])


def clean(values):
    stride = len(values) // 2
    while stride:
        for i in range(len(values)):
            if not i & stride:
                order_pair(values, i, i + stride)
        stride //= 2


def clean_block(load, store, start, count):
    values = [load(start + i) for i in range(count)]
    clean(values)
    for i in range(count):
        store(start + i, values[i])


def sort_all(load, store, load_sorted, total, block):
    for start in range(0, total, block):
        values = [load(start + i) for i in range(block)]
        for i, j in batcher(block):
            order_pair(values, i, j)
        for i in range(block):
            store(start + i, values[i])
    size = 2 * block
    while size <= total:
        for start in range(0, total, size):
            if size == 2 * block:
                upper, lower = [], []
                for i in range(block):
                    a, b = load_sorted(start + i), load_sorted(start + size - 1 - i)
                    upper.append(jnp.maximum(a, b))
                    lower.append(jnp.minimum(a, b))
                for offset, values in ((0, upper), (block, lower[::-1])):
                    clean(values)
                    for i in range(block):
                        store(start + offset + i, values[i])
            else:
                half, quarter = size // 2, size // 4
                for i in range(quarter):
                    spots = (i, i + quarter, size - 1 - i - quarter, size - 1 - i)
                    values = [load_sorted(start + spot) for spot in spots]
                    order_pair(values, 0, 3)
                    order_pair(values, 1, 2)
                    order_pair(values, 0, 1)
                    order_pair(values, 2, 3)
                    for spot, value in zip(spots, values):
                        store(start + spot, value)
                for offset in range(0, size, quarter):
                    clean_block(load_sorted, store, start + offset, quarter)
        size *= 2


def merge_top(load, store, load_merged, partner, total):
    quarter = total // 4
    done = {}
    for i in range(quarter):
        spots = [i, i + quarter, i + 2 * quarter, i + 3 * quarter]
        values = [jnp.maximum(load(spot), partner(load(total - 1 - spot))) for spot in spots]
        order_pair(values, 0, 2)
        order_pair(values, 1, 3)
        order_pair(values, 0, 1)
        order_pair(values, 2, 3)
        for spot, value in zip(spots, values):
            store(spot, value)
    for offset in range(0, total, quarter):
        clean_block(load_merged, store, offset, quarter)


def rank_kernel(scores_ref, query_ref, codes_ref, items_hbm, weight_hbm, bias_ref, out_weight_ref,
                result_ref, weight_ref, table_ref, query_f32, user_f32, pair_ref, sort_a, sort_b, best_ref,
                pick_ref, first_ref, state_ref, round_a, round_b, weight_sem, items_sem, *, fetch):
    item_rows, requests = scores_ref.shape
    weight_copy = pltpu.make_async_copy(weight_hbm, weight_ref, weight_sem)
    items_copy = pltpu.make_async_copy(items_hbm, table_ref.at[pl.ds(0, item_rows), :], items_sem)
    items_copy.start()
    weight_copy.start()
    size = codes_ref.shape[0] // SUBLANES
    local = requests // size

    query_f32[...] = query_ref[...].astype(F32)
    for i in range(EMB):
        for r in range(local):
            rows = query_f32[pl.ds(i * local + r, size, stride=local * EMB), :]
            user_f32[i, pl.ds(r, size, stride=local), :] = rows
        table_ref[item_rows:, i * D : (i + 1) * D] = user_f32[i].astype(BF16)
    pair_ref[:, :requests], pair_ref[:, requests:] = split_two(scores_ref[...])
    total = size * fetch
    block = total // BLOCKS
    width = first_ref.shape[-1]
    code_item = codes_ref[message(0, size), :]
    digits = jnp.concatenate(
        [code_item // BASE, code_item % BASE, codes_ref[message(1, size), :]], axis=1
    ).astype(F32).astype(BF16)
    answer = jnp.zeros((size, LANES), F32)

    def source_of(shape, dim, start):
        row = (iota(shape, dim) + start).astype(F32)
        return jnp.floor((row + 0.5) * (1.0 / fetch))

    def slot_of(start):
        source = source_of((block, LANES), 0, start).astype(jnp.int32)
        return iota((block, LANES), 0) + start - source * fetch == iota((block, LANES), 1)

    for part in range(BLOCKS):
        start = part * block
        pick = pick_ref.at[part]
        from_source = source_of((block, size), 0, start) == iota((block, size), 1).astype(F32)
        taken = dot(ones_where(from_source), digits)
        mine = slot_of(start)
        item = jnp.sum(
            jnp.where(mine, taken[:, :LANES] * BASE + taken[:, LANES : 2 * LANES], 0.0),
            axis=1, keepdims=True,
        ).astype(jnp.int32)
        request = jnp.sum(
            jnp.where(mine, taken[:, 2 * LANES :], 0.0), axis=1, keepdims=True
        ).astype(jnp.int32)
        pick[:, :item_rows] = ones_where(item == iota((block, item_rows), 1))
        pick[:, item_rows:] = ones_where(request == iota((block, requests), 1))

    layers = weight_ref.shape[0]
    items_copy.wait()
    for part in range(BLOCKS):
        for column in range(0, width, COLUMNS):
            columns = slice(column, column + COLUMNS)
            values = dot(pick_ref[part], table_ref[:, columns])
            first_ref[part, :, columns] = values
            round_a[part, :, columns] = values.astype(BF16)
    partial = [None] * BLOCKS
    rounded = (round_a, round_b)
    weight_copy.wait()
    for layer in range(layers):
        for part in range(BLOCKS):
            for column in range(0, width, COLUMNS):
                columns = slice(column, column + COLUMNS)
                hidden = dot(rounded[layer % 2][part], weight_ref[layer, :, columns])
                hidden = hidden + bias_ref[layer : layer + 1, columns]
                first = first_ref[part, :, columns]
                after = first * hidden + (state_ref[part, :, columns] if layer else first)
                if layer + 1 < layers:
                    state_ref[part, :, columns] = after
                    rounded[(layer + 1) % 2][part, :, columns] = after.astype(BF16)
                else:
                    weighted = after * out_weight_ref[:, columns]
                    for i in range(COLUMNS // LANES):
                        term = weighted[:, i * LANES : (i + 1) * LANES]
                        partial[part] = term if partial[part] is None else partial[part] + term
        if layer == SORT_AT:
            best_of(scores_ref, codes_ref, result_ref, sort_a, sort_b, best_ref, local)
    for part in range(BLOCKS):
        start = part * block
        mixed = dot(pick_ref[part, :, :item_rows], pair_ref[...])
        mixed = mixed[:, :requests] + mixed[:, requests:]
        mixed = mixed * pick_ref[part, :, item_rows:].astype(F32)
        total_row = partial[part]
        for i in range(requests // LANES):
            total_row = total_row + mixed[:, i * LANES : (i + 1) * LANES]
        column = jnp.sum(total_row, axis=1, keepdims=True)
        placed = jnp.where(slot_of(start), column, 0.0)
        to_source = ones_where(
            source_of((size, block), 1, start) == iota((size, block), 0).astype(F32)
        )
        high, rest = split_two(placed)
        middle, low = split_two(placed - high.astype(F32))
        answer = answer + (dot(to_source, high) + (dot(to_source, middle) + dot(to_source, low)))
    spare = LANES - KEEP
    free = iota(answer.shape, 1) >= KEEP
    for row in range(local):
        moved = pltpu.roll(answer, (KEEP - row * spare) % LANES, 1)
        result_ref[message(row, size), :] = jnp.where(free, moved, result_ref[message(row, size), :])


def best_of(scores_ref, codes_ref, result_ref, sort_a, sort_b, best_ref, local):
    size = codes_ref.shape[0] // SUBLANES
    item_rows, requests = scores_ref.shape
    lists = item_rows // EMB
    masks = codes_ref[message(2, size), :].astype(F32).astype(BF16)
    lane, from_row = iota((LANES, requests), 1), iota((LANES, requests), 0)
    source = iota((size, requests), 1) // local == iota((size, requests), 0)
    allowed = []
    for cluster in range(CL_DEV):
        spread = dot(masks, ones_where(from_row == cluster * local + lane % local))
        allowed.append(jnp.sum(jnp.where(source, spread, 0.0), axis=0, keepdims=True) > 0.5)
    for chunk in range(requests // LANES):
        lanes = slice(chunk * LANES, (chunk + 1) * LANES)
        fits = [jnp.broadcast_to(a[:, lanes], (EMB, LANES)) for a in allowed]

        def load(i):
            values = scores_ref[i * EMB : (i + 1) * EMB, lanes]
            return jnp.where(fits[i * CL_DEV // lists], values, NEVER)

        def reader(ref):
            return lambda i: ref[i]

        def writer(ref):
            def store(i, value):
                ref[i] = value
            return store

        sort_all(load, writer(sort_a), reader(sort_a), lists, 32)
        held, other = sort_a, sort_b
        shift = EMB // 2
        while shift:
            merge_top(
                reader(held), writer(other), reader(other),
                functools.partial(pltpu.roll, shift=shift, axis=0), lists,
            )
            held, other = other, held
            shift //= 2
        for i in range(lists):
            best_ref[i : i + 1, :] = held[i][:1, :]
        best_ref[...] = best_ref[...].T
        per_chunk = LANES // local
        for r in range(local):
            start = chunk * per_chunk * SUBLANES + r
            result_ref[pl.ds(start, per_chunk, stride=SUBLANES), :] = (
                best_ref[pl.ds(r, per_chunk, stride=local), :]
            )


def rank(scores, queries, items, codes, cross_weight, cross_bias, out_weight, fetch):
    requests = scores.shape[1]
    vmem = pl.BlockSpec(memory_space=pltpu.VMEM)
    item_rows, width = items.shape
    total = codes.shape[0] // SUBLANES * fetch
    block = (BLOCKS, total // BLOCKS)
    anywhere = pl.BlockSpec(memory_space=pl.ANY)
    return pl.pallas_call(
        functools.partial(rank_kernel, fetch=fetch),
        out_shape=jax.ShapeDtypeStruct(codes.shape, F32),
        in_specs=[vmem, vmem, vmem, anywhere, anywhere, vmem, vmem],
        out_specs=vmem,
        scratch_shapes=[
            pltpu.VMEM(cross_weight.shape, BF16),
            pltpu.VMEM((item_rows + requests, width), BF16),
            pltpu.VMEM(queries.shape, F32),
            pltpu.VMEM((EMB, requests, D), F32),
            pltpu.VMEM((item_rows, 2 * requests), BF16),
            pltpu.VMEM((item_rows // EMB, EMB, LANES), F32),
            pltpu.VMEM((item_rows // EMB, EMB, LANES), F32),
            pltpu.VMEM((LANES, LANES), F32),
            pltpu.VMEM((*block, item_rows + requests), BF16),
            pltpu.VMEM((*block, width), F32),
            pltpu.VMEM((*block, width), F32),
            pltpu.VMEM((*block, width), BF16),
            pltpu.VMEM((*block, width), BF16),
            pltpu.SemaphoreType.DMA,
            pltpu.SemaphoreType.DMA,
        ],
        compiler_params=pltpu.CompilerParams(vmem_limit_bytes=VMEM),
        name="rank",
    )(scores, queries, codes, items, cross_weight, cross_bias, out_weight)


def merge_kernel(back_ref, owner_ref, place_ref, top_ref, rerank_ref, list_ref):
    size = back_ref.shape[0] // SUBLANES
    local = top_ref.shape[0]
    rows = owner_ref.shape[1]
    at = owner_ref[...] == iota((size, rows), 0)
    spread = jnp.zeros((size, rows), F32)
    spare = LANES - KEEP
    for row in range(local):
        lane = iota((LANES, rows), 0)
        held = jnp.where(lane >= KEEP, lane - KEEP + row * spare, -1)
        slots = ones_where(place_ref[...] == held)
        answer = back_ref[message(row, size), :]
        high, rest = split_two(answer)
        middle, low = split_two(answer - high.astype(F32))
        spread = spread + (dot(high, slots) + (dot(middle, slots) + dot(low, slots)))
    rerank_ref[...] = jnp.sum(jnp.where(at, spread, 0.0), axis=0)

    for r in range(local):
        best = back_ref[message(r, size), :]
        list_ref[pl.ds(r, size, stride=local), :] = jnp.where(iota(best.shape, 1) < KEEP, best, NEVER)
    lists = list_ref[...].T
    while lists.shape[1] > LANES:
        half = lists.shape[1] // 2
        lists = best_of_two(lists[:, :half], lists[:, half:])
    shift = LANES // 2
    while shift >= local:
        lists = best_of_two(lists, pltpu.roll(lists, LANES - shift, 1))
        shift //= 2
    top_ref[...] = lists.T[:local, :KEEP]


def neighbour(x, distance):
    upper = (iota(x.shape, 0) & distance) == 0
    return jnp.where(upper, pltpu.roll(x, EMB - distance, 0), pltpu.roll(x, distance, 0)), upper


def best_of_two(a, b):
    count = a.shape[0] // EMB
    values = []
    for i in range(count):
        other = b[(count - 1 - i) * EMB : (count - i) * EMB, :]
        for distance in (1, 2, 4):
            other = neighbour(other, distance)[0]
        values.append(jnp.maximum(a[i * EMB : (i + 1) * EMB, :], other))
    clean(values)
    for distance in (4, 2, 1):
        for i, value in enumerate(values):
            other, upper = neighbour(value, distance)
            values[i] = jnp.where(upper, jnp.maximum(value, other), jnp.minimum(value, other))
    return jnp.concatenate(values, axis=0)


def merge(back, owner, place, local):
    size = back.shape[0] // SUBLANES
    return pl.pallas_call(
        merge_kernel,
        out_shape=(
            jax.ShapeDtypeStruct((local, KEEP), F32),
            jax.ShapeDtypeStruct(owner.shape[1:], F32),
        ),
        scratch_shapes=[
            pltpu.VMEM((size * local, LANES), F32),
        ],
        compiler_params=pltpu.CompilerParams(vmem_limit_bytes=VMEM),
        name="merge",
    )(back, owner, place)


def exchange(x):
    return lax.all_to_all(x, "cand", split_axis=0, concat_axis=0, tiled=True)


def on_device(users, items, probes, gate_weight, gate_bias, cross_weight, cross_bias, out_weight,
              row_device, row_item, row_request):
    size = lax.axis_size("cand")
    local = users.shape[0]
    rows = row_item.shape[0]
    fetch = max(2, 2 * rows // size)
    own = users.reshape(local, EMB, D).swapaxes(0, 1).reshape(1, local * EMB, D)
    queries = exchange(jnp.broadcast_to(own, (size, local * EMB, D)))
    queries = queries.reshape(size * local * EMB, D)
    owner = row_device.reshape(1, rows)
    codes, place, gate_full, bias_full = plan(
        owner, row_item.reshape(1, rows), row_request.reshape(1, rows), probes,
        gate_weight, gate_bias.reshape(1, PAIRS), size,
    )
    queries, codes = lax.optimization_barrier((queries, codes))
    codes = exchange(codes)
    scores = score(queries, items, gate_full, bias_full)
    result = rank(
        scores, queries, items, codes, cross_weight, cross_bias, out_weight.reshape(1, -1), fetch
    )
    return merge(exchange(result), owner, place, local)


def solution(mesh):
    split_rows = P(("groups", "cand"), None)
    split = P(("groups", "cand"))
    return jax.shard_map(
        on_device,
        mesh=mesh,
        in_specs=(split_rows, split_rows, split_rows, P(), P(), P(), P(), P(), split_rows, split, split),
        out_specs=(split_rows, split),
        check_vma=False,
    )
```

```python
import functools
import math

import jax
import jax.numpy as jnp
from jax import lax
from jax.experimental import pallas as pl
from jax.experimental.pallas import tpu as pltpu
from jax.sharding import PartitionSpec as P

EMB = 8
D = 128
PAIRS = EMB * EMB
PROBES = 32
KEEP = 96
CL_DEV = 2
REQ_DEV = 4
LANES = 128
SUBLANES = 4
BLOCKS = 2
SORT_AT = 2
COLUMNS = 256
NEVER = -1e30
TILE_COLS = 256
GROUP = 4
UNROLL = 32
AHEAD = 8
ROWS = 512
BASE = 32
LOG2E = math.log2(math.e)
SCALE = 1.0 / math.sqrt(D)
VMEM = 56 * 1024 * 1024

F32 = jnp.float32
BF16 = jnp.bfloat16
NT = (((1,), (1,)), ((), ()))


def iota(shape, dim):
    return lax.broadcasted_iota(jnp.int32, shape, dim)


def dot(a, b):
    return jnp.dot(a, b, preferred_element_type=F32)


def dot_nt(a, b):
    return lax.dot_general(a, b, NT, preferred_element_type=F32)


def ones_where(cond):
    return jnp.where(cond, 1.0, 0.0).astype(BF16)


def message(row, size):
    return pl.ds(row, size, stride=SUBLANES)


def tree_sum(values):
    values = [(a + b).astype(F32) for a, b in zip(values[::2], values[1::2])]
    while len(values) > 1:
        values = [a + b for a, b in zip(values[::2], values[1::2])]
    return values[0]


def split_two(x):
    high = x.astype(BF16)
    return high, (x - high.astype(F32)).astype(BF16)


def plan_kernel(owner_ref, item_ref, request_ref, probes_ref, gate_ref, bias_ref,
                codes_ref, place_ref, gate_out, bias_out):
    rows = owner_ref.shape[1]
    size = codes_ref.shape[0] // SUBLANES
    at = owner_ref[...] == iota((size, rows), 0)
    at_one = ones_where(at)
    before = ones_where(iota((rows, rows), 0) < iota((rows, rows), 1))
    rank = dot(at_one, before)
    place = jnp.sum(jnp.where(at, rank, 0.0), axis=0, keepdims=True).astype(jnp.int32)
    place_ref[...] = place
    slots = ones_where(place == iota((LANES, rows), 0))
    item = item_ref[...]
    values = (item // BASE, item % BASE, request_ref[...])
    spread = jnp.concatenate(
        [jnp.where(at, value.astype(F32), 0.0).astype(BF16) for value in values], axis=0
    )
    codes = dot_nt(spread, slots)
    codes_ref[...] = jnp.zeros_like(codes_ref)
    items = (codes[:size] * BASE + codes[size : 2 * size]).astype(jnp.int32)
    codes_ref[message(0, size), :] = items
    codes_ref[message(1, size), :] = codes[2 * size :].astype(jnp.int32)
    requests, probes = probes_ref.shape
    lane = iota((size, LANES), 1)
    masks = jnp.zeros((size, LANES), F32)
    for cluster in range(CL_DEV):
        ids = iota((size, probes), 0) * CL_DEV + cluster
        for request in range(requests):
            hit = jnp.where(probes_ref[request : request + 1, :] == ids, 1.0, 0.0)
            any_hit = jnp.max(hit, axis=1, keepdims=True)
            masks = jnp.where(lane == cluster * requests + request, any_hit, masks)
    codes_ref[message(2, size), :] = masks.astype(jnp.int32)
    side = GROUP * PAIRS
    step = GROUP * EMB
    row, col = iota((side, PAIRS), 0), iota((side, PAIRS), 1)
    select = ones_where((row % step // GROUP) * EMB + row // step == col)
    part = dot_nt(select, gate_ref[...]).astype(BF16)
    full = dot_nt(part, select)
    same = iota((side, side), 0) % GROUP == iota((side, side), 1) % GROUP
    gate_out[...] = jnp.where(same, full, 0.0).astype(BF16)
    order = (row % step // GROUP) * EMB + row // step == col
    column = jnp.sum(jnp.where(order, bias_ref[...], 0.0), axis=1, keepdims=True)
    bias_out[...] = jnp.broadcast_to(column, bias_out.shape).astype(BF16)


def plan(owner, item, request, probes, gate_weight, gate_bias, size):
    rows = owner.shape[1]
    return pl.pallas_call(
        plan_kernel,
        out_shape=(
            jax.ShapeDtypeStruct((size * SUBLANES, LANES), jnp.int32),
            jax.ShapeDtypeStruct((1, rows), jnp.int32),
            jax.ShapeDtypeStruct((GROUP * PAIRS, GROUP * PAIRS), BF16),
            jax.ShapeDtypeStruct((GROUP * PAIRS, LANES), BF16),
        ),
        compiler_params=pltpu.CompilerParams(vmem_limit_bytes=VMEM),
        name="plan",
    )(owner, item, request, probes, gate_weight, gate_bias)


def score_kernel(query_ref, items_ref, gate_ref, bias_ref, scores_ref,
                 dots_ref, num_ref, den_ref, *logits):
    query_rows = query_ref.shape[0]
    tiles = items_ref.shape[0] // TILE_COLS
    step = GROUP * EMB
    groups = query_rows // step
    units = tiles * groups

    @pl.loop(0, tiles * EMB // AHEAD)
    def _(index):
        for k in range(AHEAD):
            piece = index * AHEAD + k
            tile, j = piece // EMB, piece % EMB
            start = pl.multiple_of(tile * TILE_COLS, TILE_COLS)
            lanes = pl.multiple_of(j * D, D)
            for block in range(query_rows // ROWS):
                rows = slice(block * ROWS, (block + 1) * ROWS)
                values = dot_nt(
                    query_ref[rows, :], items_ref[pl.ds(start, TILE_COLS), pl.ds(lanes, D)]
                )
                dots_ref[tile, j, rows, :] = (values * SCALE).astype(BF16)

    def place(unit):
        unit = jnp.minimum(unit, units - 1)
        tile, group = unit // groups, unit % groups
        return tile, pl.multiple_of(group * step, step), group

    def gate(unit, out):
        tile, start, _ = place(unit)
        part = dots_ref[tile, :, pl.ds(start, step), :].reshape(GROUP * PAIRS, TILE_COLS)
        out[...] = dot(gate_ref[...], part).astype(BF16)

    def mix(unit, logits):
        tile, start, _ = place(unit)
        weights, products = [], []
        for j in range(EMB):
            bias = bias_ref[j * step : (j + 1) * step, :]
            logit = logits[j * step : (j + 1) * step, :] + jnp.concatenate([bias, bias], axis=1)
            power = jnp.exp2(jnp.minimum(logit * LOG2E, 126.0))
            weight = jnp.maximum(jnp.log(1.0 + power), logit)
            weights.append(weight)
            products.append(weight * dots_ref[tile, j, pl.ds(start, step), :])
        totals = []
        for values in (weights, products):
            both = jnp.sum(tree_sum(values).reshape(step // (2 * GROUP), 2 * GROUP, TILE_COLS), axis=0)
            totals.append(both + pltpu.roll(both, GROUP, 0))
        return totals

    def keep(unit, even, odd):
        tile, _, group = place(unit)
        rows = pl.ds(pl.multiple_of(group * GROUP, 2 * GROUP), 2 * GROUP)
        upper = iota((2 * GROUP, TILE_COLS), 0) < GROUP
        for out, a, b in zip((den_ref, num_ref), even, odd):
            out[tile, rows, :] = jnp.where(upper, a, b)

    gate(0, logits[0])
    gate(1, logits[1])

    @pl.loop(0, units // UNROLL)
    def _(index):
        for phase in range(UNROLL // 2):
            first = index * UNROLL + phase * 2
            side = 2 * (phase % 2)
            here, there = logits[side : side + 2], logits[2 - side : 4 - side]
            for k in range(2):
                gate(first + 2 + k, there[k])
            keep(first, mix(first, here[0]), mix(first + 1, here[1]))

    for tile in range(tiles):
        values = num_ref[tile] / (1.0 + den_ref[tile])
        scores_ref[tile * TILE_COLS : (tile + 1) * TILE_COLS, :] = values.T


def score(queries, items, gate_full, bias_full):
    query_rows, item_rows = queries.shape[0], items.shape[0]
    tiles = item_rows // TILE_COLS
    return pl.pallas_call(
        score_kernel,
        out_shape=jax.ShapeDtypeStruct((item_rows, query_rows // EMB), F32),
        scratch_shapes=[
            pltpu.VMEM((tiles, EMB, query_rows, TILE_COLS), BF16),
            pltpu.VMEM((tiles, query_rows // EMB, TILE_COLS), F32),
            pltpu.VMEM((tiles, query_rows // EMB, TILE_COLS), F32),
        ]
        + [pltpu.VMEM((GROUP * PAIRS, TILE_COLS), BF16) for _ in range(4)],
        compiler_params=pltpu.CompilerParams(vmem_limit_bytes=VMEM),
        name="score",
    )(queries, items, gate_full, bias_full)


def batcher(count):
    pairs = []
    p = 1
    while p < count:
        k = p
        while k >= 1:
            for j in range(k % p, count - k, 2 * k):
                for i in range(min(k, count - j - k)):
                    if (i + j) // (2 * p) == (i + j + k) // (2 * p):
                        pairs.append((i + j, i + j + k))
            k //= 2
        p *= 2
    return pairs


def order_pair(values, i, j):
    values[i], values[j] = jnp.maximum(values[i], values[j]), jnp.minimum(values[i], values[j])


def clean(values):
    stride = len(values) // 2
    while stride:
        for i in range(len(values)):
            if not i & stride:
                order_pair(values, i, i + stride)
        stride //= 2


def clean_block(load, store, start, count):
    values = [load(start + i) for i in range(count)]
    clean(values)
    for i in range(count):
        store(start + i, values[i])


def sort_all(load, store, load_sorted, total, block):
    for start in range(0, total, block):
        values = [load(start + i) for i in range(block)]
        for i, j in batcher(block):
            order_pair(values, i, j)
        for i in range(block):
            store(start + i, values[i])
    size = 2 * block
    while size <= total:
        for start in range(0, total, size):
            if size == 2 * block:
                upper, lower = [], []
                for i in range(block):
                    a, b = load_sorted(start + i), load_sorted(start + size - 1 - i)
                    upper.append(jnp.maximum(a, b))
                    lower.append(jnp.minimum(a, b))
                for offset, values in ((0, upper), (block, lower[::-1])):
                    clean(values)
                    for i in range(block):
                        store(start + offset + i, values[i])
            else:
                half, quarter = size // 2, size // 4
                for i in range(quarter):
                    spots = (i, i + quarter, size - 1 - i - quarter, size - 1 - i)
                    values = [load_sorted(start + spot) for spot in spots]
                    order_pair(values, 0, 3)
                    order_pair(values, 1, 2)
                    order_pair(values, 0, 1)
                    order_pair(values, 2, 3)
                    for spot, value in zip(spots, values):
                        store(start + spot, value)
                for offset in range(0, size, quarter):
                    clean_block(load_sorted, store, start + offset, quarter)
        size *= 2


def merge_top(load, store, load_merged, partner, total):
    quarter = total // 4
    done = {}
    for i in range(quarter):
        spots = [i, i + quarter, i + 2 * quarter, i + 3 * quarter]
        values = [jnp.maximum(load(spot), partner(load(total - 1 - spot))) for spot in spots]
        order_pair(values, 0, 2)
        order_pair(values, 1, 3)
        order_pair(values, 0, 1)
        order_pair(values, 2, 3)
        for spot, value in zip(spots, values):
            store(spot, value)
    for offset in range(0, total, quarter):
        clean_block(load_merged, store, offset, quarter)


def rank_kernel(scores_ref, query_ref, codes_ref, items_hbm, weight_hbm, bias_ref, out_weight_ref,
                result_ref, weight_ref, table_ref, query_f32, user_f32, pair_ref, sort_a, sort_b, best_ref,
                pick_ref, first_ref, state_ref, round_a, round_b, weight_sem, items_sem, *, fetch):
    item_rows, requests = scores_ref.shape
    weight_copy = pltpu.make_async_copy(weight_hbm, weight_ref, weight_sem)
    items_copy = pltpu.make_async_copy(items_hbm, table_ref.at[pl.ds(0, item_rows), :], items_sem)
    items_copy.start()
    weight_copy.start()
    size = codes_ref.shape[0] // SUBLANES
    local = requests // size

    query_f32[...] = query_ref[...].astype(F32)
    for i in range(EMB):
        for r in range(local):
            rows = query_f32[pl.ds(i * local + r, size, stride=local * EMB), :]
            user_f32[i, pl.ds(r, size, stride=local), :] = rows
        table_ref[item_rows:, i * D : (i + 1) * D] = user_f32[i].astype(BF16)
    pair_ref[:, :requests], pair_ref[:, requests:] = split_two(scores_ref[...])
    total = size * fetch
    block = total // BLOCKS
    width = first_ref.shape[-1]
    code_item = codes_ref[message(0, size), :]
    digits = jnp.concatenate(
        [code_item // BASE, code_item % BASE, codes_ref[message(1, size), :]], axis=1
    ).astype(F32).astype(BF16)
    answer = jnp.zeros((size, LANES), F32)

    def source_of(shape, dim, start):
        row = (iota(shape, dim) + start).astype(F32)
        return jnp.floor((row + 0.5) * (1.0 / fetch))

    def slot_of(start):
        source = source_of((block, LANES), 0, start).astype(jnp.int32)
        return iota((block, LANES), 0) + start - source * fetch == iota((block, LANES), 1)

    for part in range(BLOCKS):
        start = part * block
        pick = pick_ref.at[part]
        from_source = source_of((block, size), 0, start) == iota((block, size), 1).astype(F32)
        taken = dot(ones_where(from_source), digits)
        mine = slot_of(start)
        item = jnp.sum(
            jnp.where(mine, taken[:, :LANES] * BASE + taken[:, LANES : 2 * LANES], 0.0),
            axis=1, keepdims=True,
        ).astype(jnp.int32)
        request = jnp.sum(
            jnp.where(mine, taken[:, 2 * LANES :], 0.0), axis=1, keepdims=True
        ).astype(jnp.int32)
        pick[:, :item_rows] = ones_where(item == iota((block, item_rows), 1))
        pick[:, item_rows:] = ones_where(request == iota((block, requests), 1))

    layers = weight_ref.shape[0]
    items_copy.wait()
    for part in range(BLOCKS):
        for column in range(0, width, COLUMNS):
            columns = slice(column, column + COLUMNS)
            values = dot(pick_ref[part], table_ref[:, columns])
            first_ref[part, :, columns] = values
            round_a[part, :, columns] = values.astype(BF16)
    partial = [None] * BLOCKS
    rounded = (round_a, round_b)
    weight_copy.wait()
    for layer in range(layers):
        for part in range(BLOCKS):
            for column in range(0, width, COLUMNS):
                columns = slice(column, column + COLUMNS)
                hidden = dot(rounded[layer % 2][part], weight_ref[layer, :, columns])
                hidden = hidden + bias_ref[layer : layer + 1, columns]
                first = first_ref[part, :, columns]
                after = first * hidden + (state_ref[part, :, columns] if layer else first)
                if layer + 1 < layers:
                    state_ref[part, :, columns] = after
                    rounded[(layer + 1) % 2][part, :, columns] = after.astype(BF16)
                else:
                    weighted = after * out_weight_ref[:, columns]
                    for i in range(COLUMNS // LANES):
                        term = weighted[:, i * LANES : (i + 1) * LANES]
                        partial[part] = term if partial[part] is None else partial[part] + term
        if layer == SORT_AT:
            best_of(scores_ref, codes_ref, result_ref, sort_a, sort_b, best_ref, local)
    for part in range(BLOCKS):
        start = part * block
        mixed = dot(pick_ref[part, :, :item_rows], pair_ref[...])
        mixed = mixed[:, :requests] + mixed[:, requests:]
        mixed = mixed * pick_ref[part, :, item_rows:].astype(F32)
        total_row = partial[part]
        for i in range(requests // LANES):
            total_row = total_row + mixed[:, i * LANES : (i + 1) * LANES]
        column = jnp.sum(total_row, axis=1, keepdims=True)
        placed = jnp.where(slot_of(start), column, 0.0)
        to_source = ones_where(
            source_of((size, block), 1, start) == iota((size, block), 0).astype(F32)
        )
        high, rest = split_two(placed)
        middle, low = split_two(placed - high.astype(F32))
        answer = answer + (dot(to_source, high) + (dot(to_source, middle) + dot(to_source, low)))
    spare = LANES - KEEP
    free = iota(answer.shape, 1) >= KEEP
    for row in range(local):
        moved = pltpu.roll(answer, (KEEP - row * spare) % LANES, 1)
        result_ref[message(row, size), :] = jnp.where(free, moved, result_ref[message(row, size), :])


def best_of(scores_ref, codes_ref, result_ref, sort_a, sort_b, best_ref, local):
    size = codes_ref.shape[0] // SUBLANES
    item_rows, requests = scores_ref.shape
    lists = item_rows // EMB
    masks = codes_ref[message(2, size), :].astype(F32).astype(BF16)
    lane, from_row = iota((LANES, requests), 1), iota((LANES, requests), 0)
    source = iota((size, requests), 1) // local == iota((size, requests), 0)
    allowed = []
    for cluster in range(CL_DEV):
        spread = dot(masks, ones_where(from_row == cluster * local + lane % local))
        allowed.append(jnp.sum(jnp.where(source, spread, 0.0), axis=0, keepdims=True) > 0.5)
    for chunk in range(requests // LANES):
        lanes = slice(chunk * LANES, (chunk + 1) * LANES)
        fits = [jnp.broadcast_to(a[:, lanes], (EMB, LANES)) for a in allowed]

        def load(i):
            values = scores_ref[i * EMB : (i + 1) * EMB, lanes]
            return jnp.where(fits[i * CL_DEV // lists], values, NEVER)

        def reader(ref):
            return lambda i: ref[i]

        def writer(ref):
            def store(i, value):
                ref[i] = value
            return store

        sort_all(load, writer(sort_a), reader(sort_a), lists, 32)
        held, other = sort_a, sort_b
        shift = EMB // 2
        while shift:
            merge_top(
                reader(held), writer(other), reader(other),
                functools.partial(pltpu.roll, shift=shift, axis=0), lists,
            )
            held, other = other, held
            shift //= 2
        for i in range(lists):
            best_ref[i : i + 1, :] = held[i][:1, :]
        best_ref[...] = best_ref[...].T
        per_chunk = LANES // local
        for r in range(local):
            start = chunk * per_chunk * SUBLANES + r
            result_ref[pl.ds(start, per_chunk, stride=SUBLANES), :] = (
                best_ref[pl.ds(r, per_chunk, stride=local), :]
            )


def rank(scores, queries, items, codes, cross_weight, cross_bias, out_weight, fetch):
    requests = scores.shape[1]
    vmem = pl.BlockSpec(memory_space=pltpu.VMEM)
    item_rows, width = items.shape
    total = codes.shape[0] // SUBLANES * fetch
    block = (BLOCKS, total // BLOCKS)
    anywhere = pl.BlockSpec(memory_space=pl.ANY)
    return pl.pallas_call(
        functools.partial(rank_kernel, fetch=fetch),
        out_shape=jax.ShapeDtypeStruct(codes.shape, F32),
        in_specs=[vmem, vmem, vmem, anywhere, anywhere, vmem, vmem],
        out_specs=vmem,
        scratch_shapes=[
            pltpu.VMEM(cross_weight.shape, BF16),
            pltpu.VMEM((item_rows + requests, width), BF16),
            pltpu.VMEM(queries.shape, F32),
            pltpu.VMEM((EMB, requests, D), F32),
            pltpu.VMEM((item_rows, 2 * requests), BF16),
            pltpu.VMEM((item_rows // EMB, EMB, LANES), F32),
            pltpu.VMEM((item_rows // EMB, EMB, LANES), F32),
            pltpu.VMEM((LANES, LANES), F32),
            pltpu.VMEM((*block, item_rows + requests), BF16),
            pltpu.VMEM((*block, width), F32),
            pltpu.VMEM((*block, width), F32),
            pltpu.VMEM((*block, width), BF16),
            pltpu.VMEM((*block, width), BF16),
            pltpu.SemaphoreType.DMA,
            pltpu.SemaphoreType.DMA,
        ],
        compiler_params=pltpu.CompilerParams(vmem_limit_bytes=VMEM),
        name="rank",
    )(scores, queries, codes, items, cross_weight, cross_bias, out_weight)


def merge_kernel(back_ref, owner_ref, place_ref, top_ref, rerank_ref, list_ref):
    size = back_ref.shape[0] // SUBLANES
    local = top_ref.shape[0]
    rows = owner_ref.shape[1]
    at = owner_ref[...] == iota((size, rows), 0)
    spread = jnp.zeros((size, rows), F32)
    spare = LANES - KEEP
    for row in range(local):
        lane = iota((LANES, rows), 0)
        held = jnp.where(lane >= KEEP, lane - KEEP + row * spare, -1)
        slots = ones_where(place_ref[...] == held)
        answer = back_ref[message(row, size), :]
        high, rest = split_two(answer)
        middle, low = split_two(answer - high.astype(F32))
        spread = spread + (dot(high, slots) + (dot(middle, slots) + dot(low, slots)))
    rerank_ref[...] = jnp.sum(jnp.where(at, spread, 0.0), axis=0)

    for r in range(local):
        best = back_ref[message(r, size), :]
        list_ref[pl.ds(r, size, stride=local), :] = jnp.where(iota(best.shape, 1) < KEEP, best, NEVER)
    lists = list_ref[...].T
    while lists.shape[1] > LANES:
        half = lists.shape[1] // 2
        lists = best_of_two(lists[:, :half], lists[:, half:])
    shift = LANES // 2
    while shift >= local:
        lists = best_of_two(lists, pltpu.roll(lists, LANES - shift, 1))
        shift //= 2
    top_ref[...] = lists.T[:local, :KEEP]


def neighbour(x, distance):
    upper = (iota(x.shape, 0) & distance) == 0
    return jnp.where(upper, pltpu.roll(x, EMB - distance, 0), pltpu.roll(x, distance, 0)), upper


def best_of_two(a, b):
    count = a.shape[0] // EMB
    values = []
    for i in range(count):
        other = b[(count - 1 - i) * EMB : (count - i) * EMB, :]
        for distance in (1, 2, 4):
            other = neighbour(other, distance)[0]
        values.append(jnp.maximum(a[i * EMB : (i + 1) * EMB, :], other))
    clean(values)
    for distance in (4, 2, 1):
        for i, value in enumerate(values):
            other, upper = neighbour(value, distance)
            values[i] = jnp.where(upper, jnp.maximum(value, other), jnp.minimum(value, other))
    return jnp.concatenate(values, axis=0)


def merge(back, owner, place, local):
    size = back.shape[0] // SUBLANES
    return pl.pallas_call(
        merge_kernel,
        out_shape=(
            jax.ShapeDtypeStruct((local, KEEP), F32),
            jax.ShapeDtypeStruct(owner.shape[1:], F32),
        ),
        scratch_shapes=[
            pltpu.VMEM((size * local, LANES), F32),
        ],
        compiler_params=pltpu.CompilerParams(vmem_limit_bytes=VMEM),
        name="merge",
    )(back, owner, place)


def exchange(x):
    return lax.all_to_all(x, "cand", split_axis=0, concat_axis=0, tiled=True)


def on_device(users, items, probes, gate_weight, gate_bias, cross_weight, cross_bias, out_weight,
              row_device, row_item, row_request):
    size = lax.axis_size("cand")
    local = users.shape[0]
    rows = row_item.shape[0]
    fetch = max(2, 2 * rows // size)
    own = users.reshape(local, EMB, D).swapaxes(0, 1).reshape(1, local * EMB, D)
    queries = exchange(jnp.broadcast_to(own, (size, local * EMB, D)))
    queries = queries.reshape(size * local * EMB, D)
    owner = row_device.reshape(1, rows)
    codes, place, gate_full, bias_full = plan(
        owner, row_item.reshape(1, rows), row_request.reshape(1, rows), probes,
        gate_weight, gate_bias.reshape(1, PAIRS), size,
    )
    queries, codes = lax.optimization_barrier((queries, codes))
    codes = exchange(codes)
    scores = score(queries, items, gate_full, bias_full)
    result = rank(
        scores, queries, items, codes, cross_weight, cross_bias, out_weight.reshape(1, -1), fetch
    )
    return merge(exchange(result), owner, place, local)


def solution(mesh):
    split_rows = P(("groups", "cand"), None)
    split = P(("groups", "cand"))
    return jax.shard_map(
        on_device,
        mesh=mesh,
        in_specs=(split_rows, split_rows, split_rows, P(), P(), P(), P(), P(), split_rows, split, split),
        out_specs=(split_rows, split),
        check_vma=False,
    )
```
